32 devices in a mesh: pair: 16 (over z, x, core), pw: 2 (over y).
Axes of the slice: x: 2, y: 2, z: 4, core: 2. Of those that a mesh axis runs over, the one named last changes fastest.
Arguments:
- screened: bfloat16 [16, 4096, 4096], P('pair', 'pw'), may hold values from -0.09375 to 0.09375
- density: bfloat16 [16, 4096, 256], P('pair', 'pw'), may hold values from -0.75 to 0.75
- transform: bfloat16 [64, 256, 256], P('pw'), may hold values from -0.375 to 0.375
- energy: float32 [16384], P('pw'), may hold values from -1 to 1
- trial: bfloat16 [16384, 128], P('pw'), may hold values from -6 to 6
- coarse_index: int32 [64, 64, 4], P('pair', 'pw'), may hold values from 0 to 15, as said below
- interp_weight: bfloat16 [64, 64, 4], P('pair', 'pw'), may hold values from 0.1 to 1, as said below
- bands: int32 [64], replicated, may hold values from 8 to 16, as said below
Outputs:
- first_step: bfloat16 [16384, 128], P('pair')
- second_step: float32 [16384, 128], P('pw')
The draws below stay inside these ranges and needn't reach their ends.
Inputs may be any that keep to these rules, and one draw needn't show every extreme that they name: coarse_index[k, q, j] equals coarse_index[q, k, j]. interp_weight[k, q, j] equals interp_weight[q, k, j]. Some fine k-point has all 16 conduction bands live.
All inputs are finite; a program needn't handle non-finite values.
Results may differ from the reference program's by a relative error of at most 0.01.
Values may be sent and summed in bfloat16 or wider, within the bound.
No kernel may reach another device: no remote copies, remote signals or barrier semaphores. Data moves between devices by JAX's collectives and lax.ppermute only.
A program may use at most 128 MiB of HBM per device.

```python
import math
import jax
import jax.numpy as jnp
from jax import lax

PWAVES = 4096
NCOND = 16
TRANS = 256
NTRIAL = 128
NNB = 4
COARSE = 16
NFINE = 64
NH = 16384


def mirror_pairs(table):
    upper_half = (jnp.arange(NFINE)[:, None] <= jnp.arange(NFINE)[None, :])[:, :, None]
    return jnp.where(upper_half, table, jnp.transpose(table, (1, 0, 2)))


def draw_coarse_index(key, part):
    draw_one = jax.random.randint(jax.random.fold_in(key, 11), (NFINE, NFINE, NNB), 0, COARSE)
    draw_two = jax.random.randint(jax.random.fold_in(key, 12), (NFINE, NFINE, NNB), 0, COARSE)
    pair_table = mirror_pairs(jnp.minimum(draw_one, draw_two))
    pair_table = pair_table.at[0, 0, 0].set(COARSE - 1)
    pair_table = pair_table.at[0, 0, 1].set(0)
    return pair_table.astype(jnp.int32)


def draw_interp_weight(key, part):
    uniform_part = jax.random.uniform(jax.random.fold_in(key, 21), (NFINE, NFINE, NNB), jnp.float32, 0.0, 1.0)
    values = 0.25 + 0.75 * uniform_part
    return mirror_pairs(values).astype(jnp.bfloat16)


def draw_bands(key, part):
    counts = jax.random.randint(jax.random.fold_in(key, 31), (NFINE,), NCOND // 2, NCOND + 1)
    full_spot = jax.random.randint(jax.random.fold_in(key, 32), (), 0, NFINE)
    return counts.at[full_spot].set(NCOND).astype(jnp.int32)


def level_of(key, extent, pieces, smallest, largest):
    def one(axis_at, blocks):
        draws = jax.random.uniform(jax.random.fold_in(jax.random.fold_in(key, 6), axis_at), (blocks,), jnp.float32, smallest / len(pieces), largest / len(pieces))
        return jnp.repeat(jnp.exp(draws), extent[axis_at] // blocks).reshape((-1,) + (1,) * (len(extent) - axis_at - 1))

    gain = one(*pieces[0])
    for cut in pieces[1:]:
        gain = gain * one(*cut)
    return gain


def noise(own_key, dims, spread, limit, cuts=(), kind=jnp.bfloat16):
    values = jax.random.normal(own_key, dims, jnp.float32) * spread
    if len(cuts) > 0:
        values = level_of(own_key, dims, cuts, -0.22, 0.18) * values
    return jnp.clip(values, min=-limit, max=limit).astype(kind)


def setup_inputs(seed: int = 0) -> dict:
    streams_of = jax.random.split(jax.random.key(seed), 9)
    screened = noise(streams_of[0], (COARSE, PWAVES, PWAVES), PWAVES ** -0.5, 0.09375, ((0, 16), (1, 2)))
    density = noise(streams_of[1], (COARSE, PWAVES, TRANS), 0.125, 0.75, ((0, 16), (1, 2)))
    transform = noise(streams_of[2], (NFINE, TRANS, TRANS), TRANS ** -0.5, 0.375, ((0, 2),))
    energy = jnp.clip(jax.random.uniform(streams_of[3], (NH,), jnp.float32, -1.0, 1.0) * level_of(streams_of[3], (NH,), ((0, 2),), -0.4, 0.0), -1.0, 1.0)
    trial = noise(streams_of[4], (NH, NTRIAL), 1.0, 6.0, ((0, 2),))
    coarse_index = draw_coarse_index(jax.random.fold_in(streams_of[8], 71), 0)
    interp_weight = draw_interp_weight(jax.random.fold_in(streams_of[8], 71), 0)
    bands = draw_bands(jax.random.fold_in(streams_of[8], 71), 0)
    return {"screened": screened, "density": density, "transform": transform, "energy": energy, "trial": trial, "coarse_index": coarse_index, "interp_weight": interp_weight, "bands": bands}


def coarse_block(operands):
    screened_one, density_one = operands
    applied = jnp.dot(screened_one, density_one, preferred_element_type=jnp.float32).astype(jnp.bfloat16)
    raw_sum = jnp.dot(density_one.T, applied, preferred_element_type=jnp.float32)
    return (0.5 * (raw_sum + raw_sum.T)).astype(jnp.bfloat16)

def reference(screened, density, transform, energy, trial, coarse_index, interp_weight, bands):
    kernel = lax.map(coarse_block, (screened, density))
    live_mask = ((jnp.arange(TRANS) % NCOND)[None, :] < bands[:, None]).astype(jnp.float32)
    norm_scale = 1.0 / math.sqrt(NFINE * TRANS)
    energies = energy.reshape(NFINE, TRANS)
    identity = jnp.eye(TRANS, dtype=jnp.float32)
    transform_wide = transform.astype(jnp.float32)

    def row_block(point):
        neighbours = coarse_index[point]
        picked = kernel[neighbours].astype(jnp.float32)
        mixture = jnp.einsum('bj,bjst->bst', interp_weight[point].astype(jnp.float32), picked).astype(jnp.bfloat16)
        turned = jnp.einsum('bst,btu->bsu', mixture.astype(jnp.float32), transform_wide).astype(jnp.bfloat16)
        blocks = jnp.einsum('sv,bsu->vbu', transform_wide[point], turned.astype(jnp.float32))
        blocks = blocks * live_mask[point][:, None, None] * live_mask[None, :, :] * norm_scale
        same_point = (jnp.arange(NFINE) == point).astype(jnp.float32)
        diagonal_part = identity[:, None, :] * (energies * same_point[:, None])[None, :, :]
        return (blocks + diagonal_part).astype(jnp.bfloat16).reshape(TRANS, NFINE * TRANS)
    hamiltonian = lax.map(row_block, jnp.arange(NFINE)).reshape(NFINE * TRANS, NFINE * TRANS)
    first_step = jnp.dot(hamiltonian, trial, preferred_element_type=jnp.float32).astype(jnp.bfloat16)
    second_step = 2.0 * jnp.dot(hamiltonian.T, first_step, preferred_element_type=jnp.float32) - trial.astype(jnp.float32)
    return (first_step, second_step)
```

```python
import math

import jax
import jax.numpy as jnp
from jax import lax
from jax.sharding import PartitionSpec as P

NCOND = 16
F32 = jnp.float32
BF16 = jnp.bfloat16


def from_ahead(value, axis, step):
    count = lax.axis_size(axis)
    return lax.ppermute(value, axis, [((s + step) % count, s) for s in range(count)])


def flipped(value, axis, bit):
    count = lax.axis_size(axis)
    return lax.ppermute(value, axis, [(s, s ^ bit) for s in range(count)])


def plane_blocks(value):
    return [value] + [from_ahead(value, "pw", d) for d in range(1, lax.axis_size("pw"))]


def pair_blocks(value):
    count = lax.axis_size("pair")
    far = [value] + [from_ahead(value, "pair", 4 * d) for d in range(1, count // 4)]
    side = far + [flipped(block, "pair", 2) for block in far]
    return side + [flipped(block, "pair", 1) for block in side]


def pair_order():
    count = lax.axis_size("pair")
    me = lax.axis_index("pair")
    steps = jnp.arange(count // 4)
    far = (me + 4 * steps) % count
    side = jnp.concatenate([far, far ^ 2])
    return jnp.concatenate([side, side ^ 1])


def plane_sum(value):
    blocks = plane_blocks(value)
    if len(blocks) == 2:
        return blocks[0].astype(F32) + blocks[1].astype(F32)
    stacked = jnp.roll(jnp.stack(blocks), lax.axis_index("pw"), axis=0)
    return jnp.sum(stacked.astype(F32), axis=0)


def shards(screened, density, transform, energy, trial, coarse_index, interp_weight, bands):
    pair_count = lax.axis_size("pair")
    plane_count = lax.axis_size("pw")
    row_index = lax.axis_index("pair")
    col_index = lax.axis_index("pw")
    rows_here = density.shape[1]
    transitions = density.shape[2]
    row_points = coarse_index.shape[0]
    col_points = coarse_index.shape[1]
    fine_points = bands.shape[0]
    columns = trial.shape[1]
    mine = columns // pair_count
    norm_scale = 1.0 / math.sqrt(fine_points * transitions)

    table = jnp.concatenate([coarse_index.astype(BF16), interp_weight], axis=2)
    table = lax.all_gather(table.reshape(row_points, -1), "pair", axis=0, tiled=True)
    table = table.reshape(fine_points, col_points, -1)
    table = jnp.roll(table, -col_index * col_points, axis=0)
    neighbours = coarse_index.shape[2]
    order = pair_order().astype(F32)

    def coefficients(index, weight):
        hit = index.astype(F32)[..., None, :] == order[:, None]
        return jnp.sum(jnp.where(hit, weight.astype(F32)[..., None, :], 0.0), axis=-1)

    mix = coefficients(table[..., :neighbours], table[..., neighbours:])
    mix = jnp.transpose(mix, (2, 1, 0)).astype(BF16)
    widen = (
        jnp.arange(fine_points)[:, None] == jnp.arange(fine_points * mine)[None, :] // mine
    ).astype(BF16)
    wide = jnp.einsum("ckq,qm->ckm", mix, widen, preferred_element_type=F32).astype(BF16)
    same_column = jnp.arange(mine)[:, None] == (jnp.arange(fine_points * mine) % mine)[None, :]
    mixer = jnp.where(same_column[None, None], wide[:, :, None, :], 0).reshape(
        pair_count, col_points * mine, fine_points * mine
    )

    positions = jnp.arange(transitions) % NCOND
    live = (positions[None, :] < bands[:, None]).astype(F32)
    my_live = lax.dynamic_slice_in_dim(live, col_index * col_points, col_points, 0)
    energies = energy.reshape(col_points, transitions)
    trial_blocks = trial.reshape(col_points, transitions, columns)
    pick = (
        jnp.arange(columns)[None, :] == row_index * mine + jnp.arange(mine)[:, None]
    ).astype(BF16)
    my_trial = jnp.einsum("nm,qum->qnu", pick, trial_blocks, preferred_element_type=F32)

    def turn(vectors):
        return jnp.einsum("qnu,qtu->qnt", vectors, transform, preferred_element_type=F32)

    def turn_back(vectors):
        return jnp.einsum("qns,qsv->qnv", vectors, transform, preferred_element_type=F32)

    density_blocks = plane_blocks(density[0])
    start = turn((my_trial * my_live[:, None, :]).astype(BF16)).astype(BF16)
    start = jnp.concatenate(plane_blocks(start), axis=0)

    def mixed(vectors):
        return jnp.einsum(
            "crm,mt->crt", mixer, vectors.reshape(-1, transitions), preferred_element_type=F32
        ).astype(BF16)

    first_mixed = mixed(start)

    all_start = jnp.einsum(
        "qtu,qun->qnt",
        transform,
        (trial_blocks * my_live[:, :, None]).astype(BF16),
        preferred_element_type=F32,
    ).astype(BF16)
    row_mix = coefficients(coarse_index, interp_weight).astype(BF16)
    row_mixed = jnp.einsum("kqc,qnt->cknt", row_mix, all_start, preferred_element_type=F32)
    row_mixed = row_mixed.astype(BF16).reshape(pair_count, row_points * columns, transitions)
    first_point = row_index * row_points
    wanted = lax.dynamic_slice_in_dim(transform, first_point % col_points, row_points, 0)
    wanted_blocks = plane_blocks(wanted)
    root = first_point // col_points
    row_transform = wanted
    for step in range(1, plane_count):
        from_root = (col_index + step) % plane_count == root
        row_transform = jnp.where(from_root, wanted_blocks[step], row_transform)

    applied = 0.0
    for step in range(plane_count):
        at = ((col_index + step) % plane_count) * rows_here
        block = lax.dynamic_slice_in_dim(screened[0], at, rows_here, 1)
        applied = applied + jnp.dot(block, density_blocks[step], preferred_element_type=F32)
    raw_sum = lax.dot_general(
        density[0], applied.astype(BF16), (((0,), (0,)), ((), ())), preferred_element_type=F32
    )
    symmetric = (0.5 * (raw_sum + raw_sum.T)).astype(BF16)
    kernel = plane_sum(symmetric).astype(BF16)
    kernels = jnp.stack(pair_blocks(kernel))

    def through(vectors):
        return jnp.einsum("crt,cts->rs", vectors, kernels, preferred_element_type=F32)

    back = through(first_mixed).astype(BF16).reshape(col_points, mine, transitions)
    first = turn_back(back) * norm_scale * my_live[:, None, :] + energies[:, None, :] * my_trial
    first = first.astype(BF16)
    again = turn((first * my_live[:, None, :]).astype(BF16)).astype(BF16)
    again = jnp.concatenate(plane_blocks(again), axis=0)

    row_back = through(row_mixed).astype(BF16).reshape(row_points, columns, transitions)
    row_part = jnp.einsum("ksv,kns->kvn", row_transform, row_back, preferred_element_type=F32)
    row_live = lax.dynamic_slice_in_dim(live, first_point, row_points, 0)
    row_energy = lax.dynamic_slice_in_dim(energies, first_point % col_points, row_points, 0)
    row_trial = lax.dynamic_slice_in_dim(trial_blocks, first_point % col_points, row_points, 0)
    diagonal = jnp.where(root == col_index, row_energy[:, :, None] * row_trial.astype(F32), 0.0)
    row_part = row_part * norm_scale * row_live[:, :, None] + diagonal
    first_step = plane_sum(row_part.astype(BF16)).astype(BF16)
    first_step = first_step.reshape(row_points * transitions, columns)

    back = through(mixed(again)).astype(BF16).reshape(col_points, mine, transitions)
    second = turn_back(back) * norm_scale * my_live[:, None, :] + energies[:, None, :] * first
    blocks = jnp.stack(pair_blocks(second.astype(BF16)))
    place = jnp.zeros((pair_count,), jnp.int32).at[pair_order()].set(jnp.arange(pair_count))
    blocks = blocks[place]
    whole = jnp.transpose(blocks, (1, 3, 0, 2)).reshape(-1, columns).astype(F32)
    second_step = 2.0 * whole - trial.astype(F32)
    return (first_step, second_step)


def solution(mesh):
    in_specs = (
        P("pair", "pw", None),
        P("pair", "pw", None),
        P("pw", None, None),
        P("pw"),
        P("pw", None),
        P("pair", "pw", None),
        P("pair", "pw", None),
        P(),
    )
    out_specs = (P("pair", None), P("pw", None))
    return jax.shard_map(shards, mesh=mesh, in_specs=in_specs, out_specs=out_specs, check_vma=False)
```

```python
import functools
import math

import jax
import jax.numpy as jnp
from jax import lax
from jax.experimental import pallas as pl
from jax.experimental.pallas import tpu as pltpu
from jax.sharding import PartitionSpec as P

NCOND = 16
F32 = jnp.float32
BF16 = jnp.bfloat16
MIB = 1 << 20
NN = (((1,), (0,)), ((), ()))
NT = (((1,), (1,)), ((), ()))
TN = (((0,), (0,)), ((), ()))


def dot(a, b, dims=NN):
    return lax.dot_general(a, b, dims, preferred_element_type=F32)


def cost(flops, read):
    return pl.CostEstimate(flops=int(flops), bytes_accessed=int(read), transcendentals=0)


def params(mib):
    return pltpu.CompilerParams(vmem_limit_bytes=mib * MIB)


def whole(shape):
    return pl.BlockSpec(shape, lambda *_: (0,) * len(shape))


ANY = pl.BlockSpec(memory_space=pl.ANY)


def from_ahead(value, axis, step):
    count = lax.axis_size(axis)
    return lax.ppermute(value, axis, [((s + step) % count, s) for s in range(count)])


def flipped(value, axis, bit):
    count = lax.axis_size(axis)
    return lax.ppermute(value, axis, [(s, s ^ bit) for s in range(count)])


def plane_blocks(value):
    return [value] + [from_ahead(value, "pw", d) for d in range(1, lax.axis_size("pw"))]


def pair_moves():
    groups = lax.axis_size("pair") // 4
    far = sorted(range(groups), key=lambda d: min(d, groups - d))
    early = [(d, 0, 0) for d in far] + [(0, 1, 0)] + [(d, 0, 1) for d in far] + [(0, 1, 1)]
    early += [(d, 1, 0) for d in far[1:-1]]
    late = [(d, 1, 1) for d in far[1:-1]] + [(far[-1], 1, 0), (far[-1], 1, 1)]
    return early, late


def pair_blocks(value):
    early, late = pair_moves()
    held = {(0, 0, 0): value}
    for move in early + late:
        far, side, core = move
        if core:
            held[move] = flipped(held[far, side, 0], "pair", 1)
        elif side:
            held[move] = flipped(held[far, 0, 0], "pair", 2)
        elif far:
            held[move] = from_ahead(value, "pair", 4 * far)
    return [held[move] for move in early + late]


def pair_order():
    early, late = pair_moves()
    me = lax.axis_index("pair")
    count = lax.axis_size("pair")
    return jnp.stack([((me + 4 * far) % count) ^ (2 * side + core) for far, side, core in early + late])


def small_pair_blocks(value):
    count = lax.axis_size("pair")
    me = lax.axis_index("pair")
    far = jnp.stack([value] + [from_ahead(value, "pair", 4 * d) for d in range(1, count // 4)])
    side = jnp.concatenate([far, flipped(far, "pair", 2)])
    names = (me + 4 * jnp.arange(count // 4)) % count
    names = jnp.concatenate([names, names ^ 2])
    return jnp.concatenate([side, flipped(side, "pair", 1)]), jnp.concatenate([names, names ^ 1])


def plane_sum(value):
    blocks = plane_blocks(value)
    if len(blocks) == 2:
        return blocks[0].astype(F32) + blocks[1].astype(F32)
    stacked = jnp.roll(jnp.stack(blocks), lax.axis_index("pw"), axis=0)
    return jnp.sum(stacked.astype(F32), axis=0)


def iotas(rows, cols):
    return (
        lax.broadcasted_iota(jnp.int32, (rows, cols), 0),
        lax.broadcasted_iota(jnp.int32, (rows, cols), 1),
    )


def pack(symmetric, out):
    half = symmetric.shape[0] // 2
    row, col = iotas(half, half)
    upper, lower = symmetric[:half, :half], symmetric[half:, half:]
    diagonal = jnp.sum(jnp.where(row == col, upper, 0.0), axis=0, keepdims=True)
    out[:half] = symmetric[:half, half:].astype(BF16)
    out[half : 2 * half] = jnp.where(row > col, upper, lower).astype(BF16)
    out[2 * half :] = jnp.broadcast_to(diagonal, (16, half)).astype(BF16)


def unpack(packed):
    half = packed.shape[1]
    row, col = iotas(half, half)
    corner = packed[:half]
    both = packed[half : 2 * half].astype(F32)
    diagonal = packed[2 * half : 2 * half + 1].astype(F32)
    other = both.T
    upper = jnp.where(row > col, both, jnp.where(row == col, diagonal, other))
    lower = jnp.where(row <= col, both, other)
    top = jnp.concatenate([upper.astype(BF16), corner], axis=1)
    bottom = jnp.concatenate([corner.T, lower.astype(BF16)], axis=1)
    return jnp.concatenate([top, bottom], axis=0)


def left_kernel(plane, screened, density, out, total, turned):
    step = pl.program_id(0)
    size = out.shape[1]
    rows = density.shape[0]
    per_plane = max(rows // size, 1)

    @pl.when(step == 0)
    def _():
        turned[...] = density[...].T
        total[...] = jnp.zeros_like(total)

    part = dot(turned[...], screened[0]).astype(BF16)
    out[...] = part

    @pl.when(step // per_plane == plane[0])
    def _():
        at = pl.multiple_of((step % per_plane) * size, size)
        total[...] += dot(part, density[pl.ds(at, size), :])


def left_product(plane, screened, density):
    rows, width = density.shape
    depth = screened.shape[2]
    step = min(rows, 512)
    return pl.pallas_call(
        left_kernel,
        grid_spec=pltpu.PrefetchScalarGridSpec(
            num_scalar_prefetch=1,
            grid=(depth // step,),
            in_specs=[
                pl.BlockSpec((1, rows, step), lambda g, p: (0, 0, g)),
                pl.BlockSpec((rows, width), lambda g, p: (0, 0)),
            ],
            out_specs=[
                pl.BlockSpec((width, step), lambda g, p: (0, g)),
                pl.BlockSpec((width, width), lambda g, p: (0, 0)),
            ],
            scratch_shapes=[pltpu.VMEM((width, rows), BF16)],
        ),
        out_shape=[
            jax.ShapeDtypeStruct((width, depth), BF16),
            jax.ShapeDtypeStruct((width, width), F32),
        ],
        compiler_params=params(56),
        cost_estimate=cost(2 * rows * depth * width, 2 * rows * depth),
        name="left_product",
    )(plane, screened, density)


def coarse_kernel(planes, left, total, *refs):
    *blocks, out = refs
    raw = total[...]
    for step, block in enumerate(blocks):
        rows = block.shape[0]
        at = pl.multiple_of(planes[step] * rows, rows)
        raw = raw + dot(left[:, pl.ds(at, rows)], block[...])
    pack(0.5 * (raw + raw.T), out)


def coarse_block(planes, left, total, density_blocks):
    width = left.shape[0]
    vmem = pl.BlockSpec(memory_space=pltpu.VMEM)
    return pl.pallas_call(
        coarse_kernel,
        in_specs=[pl.BlockSpec(memory_space=pltpu.SMEM)] + [vmem] * (2 + len(density_blocks)),
        out_specs=vmem,
        out_shape=jax.ShapeDtypeStruct((width + 16, width // 2), BF16),
        compiler_params=params(16),
        cost_estimate=cost(2 * width * width * left.shape[1] // 2, 4 * MIB),
        name="coarse_block",
    )(planes, left, total, *density_blocks)


def spread_parts(rows, cols, each, repeat, widen, same):
    row, at = iotas(rows * each, rows)
    repeat[...] = jnp.where((row >= at * each) & (row < (at + 1) * each), 1.0, 0.0).astype(BF16)
    at, col = iotas(cols, cols * each)
    widen[...] = jnp.where((col >= at * each) & (col < (at + 1) * each), 1.0, 0.0).astype(BF16)
    row, col = iotas(rows * each, cols * each)
    same[...] = jnp.where(row % each == col % each, 1.0, 0.0)


def spread_table(table, repeat, widen, same):
    wide = dot(dot(repeat[...], table).astype(BF16), widen[...])
    return (wide * same[...]).astype(BF16)


def mix_kernel(each, mix, *refs):
    *blocks, _, mixer, mixed, repeat, widen, same = refs

    @pl.when(pl.program_id(0) == 0)
    def _():
        spread_parts(mix.shape[1], mix.shape[2], each, repeat, widen, same)

    for c in range(mix.shape[0]):
        table = spread_table(mix[c], repeat, widen, same)
        mixer[c] = table
        total, at = 0.0, 0
        for block in blocks:
            depth = block.shape[0]
            total = total + dot(table[:, at : at + depth], block[...])
            at += depth
        mixed[c] = total.astype(BF16)


def mix_all(mix, blocks, each, after):
    count, points, fine = mix.shape
    depth, width = blocks[0].shape
    group = 4
    return pl.pallas_call(
        functools.partial(mix_kernel, each),
        grid=(count // group,),
        in_specs=[pl.BlockSpec((group, points, fine), lambda c: (c, 0, 0))]
        + [pl.BlockSpec((depth, width), lambda c: (0, 0)) for _ in blocks]
        + [ANY],
        out_specs=[
            pl.BlockSpec((group, points * each, fine * each), lambda c: (c, 0, 0)),
            pl.BlockSpec((group, points * each, width), lambda c: (c, 0, 0)),
        ],
        out_shape=[
            jax.ShapeDtypeStruct((count, points * each, fine * each), BF16),
            jax.ShapeDtypeStruct((count, points * each, width), BF16),
        ],
        scratch_shapes=[
            pltpu.VMEM((points * each, points), BF16),
            pltpu.VMEM((fine, fine * each), BF16),
            pltpu.VMEM((points * each, fine * each), F32),
        ],
        compiler_params=params(24),
        cost_estimate=cost(4 * count * points * fine * each * each * width, 8 * MIB),
        name="mix_all",
    )(mix, *blocks, after)


def row_mix_kernel(each, mix, vectors, _, out, table, repeat, widen, same):
    points, group, width = vectors.shape
    count, rows = out.shape[:2]

    @pl.when(pl.program_id(0) == 0)
    def _():
        spread_parts(mix.shape[0], mix.shape[1], each, repeat, widen, same)
        table[...] = spread_table(mix[...], repeat, widen, same)

    value = vectors[...].astype(F32).reshape(points, group // each, each, width)
    parts = []
    for g in range(group // each):
        flat = value[:, g].reshape(points * each, width).astype(BF16)
        parts.append(dot(table[...], flat).reshape(count * rows, each, width))
    joined = jnp.concatenate(parts, axis=1).astype(BF16)
    out[...] = joined.reshape(out.shape)


def row_mix_all(mix, vectors, after):
    count, rows, points = mix.shape
    columns, width = vectors.shape[1:]
    each, group = 8, 16
    return pl.pallas_call(
        functools.partial(row_mix_kernel, each),
        grid=(columns // group,),
        in_specs=[
            whole((count * rows, points)),
            pl.BlockSpec((points, group, width), lambda g: (0, g, 0)),
            ANY,
        ],
        out_specs=pl.BlockSpec((count, rows, group, width), lambda g: (0, 0, g, 0)),
        out_shape=jax.ShapeDtypeStruct((count, rows, columns, width), BF16),
        scratch_shapes=[
            pltpu.VMEM((count * rows * each, points * each), BF16),
            pltpu.VMEM((count * rows * each, count * rows), BF16),
            pltpu.VMEM((points, points * each), BF16),
            pltpu.VMEM((count * rows * each, points * each), F32),
        ],
        compiler_params=params(24),
        cost_estimate=cost(2 * count * rows * each * points * columns * width, 8 * MIB),
        name="row_mix_all",
    )(mix.reshape(count * rows, points), vectors, after)


def row_through_kernel(vectors, *refs):
    *kernels, _, out = refs
    total, c = 0.0, 0
    for kernel in kernels:
        for k in range(kernel.shape[0]):
            total = total + dot(vectors[c], kernel[k])
            c += 1
    out[...] = total.astype(BF16)


def row_through(vectors, kernels, after):
    count, rows, width = vectors.shape
    vmem = pl.BlockSpec(memory_space=pltpu.VMEM)
    return pl.pallas_call(
        row_through_kernel,
        in_specs=[vmem] * (1 + len(kernels)) + [ANY],
        out_specs=vmem,
        out_shape=jax.ShapeDtypeStruct((rows, width), BF16),
        compiler_params=params(24),
        cost_estimate=cost(2 * count * rows * width * width, 6 * MIB),
        name="row_through",
    )(vectors, *kernels, after)


def start_kernel(each, pick, transform, trial, live, start, mine, my_trial, held):
    points, width, _ = transform.shape
    for k in range(points):
        here = slice(k * each, (k + 1) * each)
        block = trial[k * width : (k + 1) * width, :]
        my_trial[here] = dot(pick[...], block, NT)
        vectors = block.astype(F32).T * live[k : k + 1, :]
        turned = dot(vectors.astype(BF16), transform[k], NT).astype(BF16)
        start[k] = turned
        held[here] = dot(pick[...], turned)
    mine[...] = held[...].astype(BF16)


def start_call(pick, transform, trial, live):
    each, columns = pick.shape
    points, width, _ = transform.shape
    group = 8
    my_rows = pl.BlockSpec((group * each, width), lambda s: (s, 0))
    return pl.pallas_call(
        functools.partial(start_kernel, each),
        grid=(points // group,),
        in_specs=[
            whole((each, columns)),
            pl.BlockSpec((group, width, width), lambda s: (s, 0, 0)),
            pl.BlockSpec((group * width, columns), lambda s: (s, 0)),
            pl.BlockSpec((group, width), lambda s: (s, 0)),
        ],
        out_specs=[
            pl.BlockSpec((group, columns, width), lambda s: (s, 0, 0)),
            my_rows,
            my_rows,
        ],
        out_shape=[
            jax.ShapeDtypeStruct((points, columns, width), BF16),
            jax.ShapeDtypeStruct((points * each, width), BF16),
            jax.ShapeDtypeStruct((points * each, width), F32),
        ],
        scratch_shapes=[pltpu.VMEM((group * each, width), F32)],
        compiler_params=params(24),
        cost_estimate=cost(4 * points * columns * width * width, 8 * MIB),
        name="start_call",
    )(pick, transform, trial, live)


def fold_kernel(scale, each, transform, live, energy, my_trial, _, folded, shift):
    for k in range(transform.shape[0]):
        here = slice(k * each, (k + 1) * each)
        table = transform[k]
        masked = (table.astype(F32) * (scale * live[k : k + 1, :])).astype(BF16)
        folded[k] = dot(masked, table, NT).astype(BF16)
        vectors = my_trial[here] * (live[k : k + 1, :] * energy[k : k + 1, :])
        shift[here] = dot(vectors.astype(BF16), table, NT)


def fold_call(transform, live, energy, my_trial, scale, each, after):
    points, width, _ = transform.shape
    group = 8
    my_rows = pl.BlockSpec((group * each, width), lambda s: (s, 0))
    point_rows = pl.BlockSpec((group, width), lambda s: (s, 0))
    tables = pl.BlockSpec((group, width, width), lambda s: (s, 0, 0))
    return pl.pallas_call(
        functools.partial(fold_kernel, scale, each),
        grid=(points // group,),
        in_specs=[tables, point_rows, point_rows, my_rows, ANY],
        out_specs=[tables, my_rows],
        out_shape=[
            jax.ShapeDtypeStruct((points, width, width), BF16),
            jax.ShapeDtypeStruct((points * each, width), F32),
        ],
        compiler_params=params(24),
        cost_estimate=cost(3 * points * width * width * width, 8 * MIB),
        name="fold_call",
    )(transform, live, energy, my_trial, after)


def by_point(each, points, body, store):
    step = max(each, 8)
    group = step // each
    owner = lax.broadcasted_iota(jnp.int32, (step, 1), 0) // each
    for b in range(points // group):
        here = slice(b * step, (b + 1) * step)
        if group == 1:
            value = body(here, b)
        else:
            value = 0.0
            for p in range(group):
                value = value + jnp.where(owner == p, body(here, b * group + p), 0.0)
        store[here] = value


def through_kernel(first, count, each, last, *refs):
    mixed_at, *refs = refs
    packed, refs = refs[:count], refs[count:]
    if last:
        before, folded_at, shift, kernels, total, again, mixed, sems, folded, held = refs
    else:
        kernels, total, mixed, sems = refs
    load = pltpu.make_async_copy(mixed_at.at[pl.ds(first, count)], mixed, sems.at[0])
    load.start()
    if last:
        load_folded = pltpu.make_async_copy(folded_at, folded, sems.at[1])
        load_folded.start()
    for c in range(count):
        kernels[c] = unpack(packed[c][...])
    load.wait()
    value = before[...] if last else 0.0
    for c in range(count):
        value = value + dot(mixed[c], kernels[c])
    total[...] = value
    if last:
        load_folded.wait()

        def body(here, k):
            return dot(total[here].astype(BF16), folded[k]) + shift[here]

        by_point(each, folded.shape[0], body, held)
        again[...] = held[...].astype(BF16)


def through(mixed, first, packed, each, before=None, folded=None, shift=None):
    _, rows, width = mixed.shape
    count = len(packed)
    last = before is not None
    vmem = pl.BlockSpec(memory_space=pltpu.VMEM)
    rows_f32 = jax.ShapeDtypeStruct((rows, width), F32)
    out_shape = [jax.ShapeDtypeStruct((count, width, width), BF16), rows_f32]
    scratch = [pltpu.VMEM((count, rows, width), BF16), pltpu.SemaphoreType.DMA((2,))]
    operands = [mixed, *packed]
    in_specs = [ANY] + [vmem] * count
    if last:
        out_shape.append(jax.ShapeDtypeStruct((rows, width), BF16))
        scratch += [pltpu.VMEM(folded.shape, BF16), pltpu.VMEM((rows, width), F32)]
        operands += [before, folded, shift]
        in_specs += [vmem, ANY, vmem]
    return pl.pallas_call(
        functools.partial(through_kernel, first, count, each, last),
        in_specs=in_specs,
        out_specs=[vmem] * len(out_shape),
        out_shape=out_shape,
        scratch_shapes=scratch,
        compiler_params=params(24),
        cost_estimate=cost(8 * count * rows * width * width, 8 * MIB),
        name="through_last" if last else "through_early",
    )(*operands)


def energy_kernel(scale, each, transform_at, total, live, energy, trial, _, out, transform, sem):
    load = pltpu.make_async_copy(transform_at, transform, sem)
    load.start()
    load.wait()

    def body(here, k):
        turned = dot(total[here].astype(BF16), transform[k])
        row = energy[k : k + 1, :]
        value = turned * (scale * live[k : k + 1, :]) + row * trial[here]
        return value * row

    by_point(each, transform.shape[0], body, out)


def energy_call(transform, total, live, energy, my_trial, scale, each, after):
    rows, width = total.shape
    vmem = pl.BlockSpec(memory_space=pltpu.VMEM)
    return pl.pallas_call(
        functools.partial(energy_kernel, scale, each),
        in_specs=[ANY] + [vmem] * 4 + [ANY],
        out_specs=vmem,
        out_shape=jax.ShapeDtypeStruct((rows, width), F32),
        scratch_shapes=[pltpu.VMEM(transform.shape, BF16), pltpu.SemaphoreType.DMA],
        compiler_params=params(24),
        cost_estimate=cost(2 * rows * width * width, 5 * MIB),
        name="energy_call",
    )(transform, total, live, energy, my_trial, after)


def step_kernel(scale, at, each, group, parts, last, mixer_at, vectors, *refs):
    kernel_refs, refs = refs[:parts], refs[parts:]
    if last:
        before, transform_at, live, shift, out, mixer, sems, transform, total, held = refs
    else:
        out, mixer, sems = refs
    depth = vectors.shape[0]
    loads = []
    for g in range(mixer.shape[0] // group):
        part = pl.ds(g * group, group)
        loads.append(
            pltpu.make_async_copy(
                mixer_at.at[part, :, pl.ds(at * depth, depth)], mixer.at[part], sems.at[g]
            )
        )
        loads[-1].start()
    if last:
        load = pltpu.make_async_copy(transform_at, transform, sems.at[len(loads)])
        load.start()
    kernels = [(ref, c) for ref in kernel_refs for c in range(ref.shape[0])]
    value = before[...] if last else 0.0
    for c, (ref, k) in enumerate(kernels):
        if c % group == 0:
            loads[c // group].wait()
        value = value + dot(dot(mixer[c], vectors[...]).astype(BF16), ref[k])
    if not last:
        out[...] = value
        return
    total[...] = value
    load.wait()

    def body(here, k):
        turned = dot(total[here].astype(BF16), transform[k])
        return turned * (scale * live[k : k + 1, :]) + shift[here]

    by_point(each, transform.shape[0], body, held)
    out[...] = held[...].astype(BF16)


def step_call(mixer, vectors, at, kernels, scale, each, last=None):
    count, rows, _ = mixer.shape
    depth, width = vectors.shape
    group = 4
    vmem = pl.BlockSpec(memory_space=pltpu.VMEM)
    sems = count // group + (last is not None)
    scratch = [pltpu.VMEM((count, rows, depth), BF16), pltpu.SemaphoreType.DMA((sems,))]
    operands = [mixer, vectors, *kernels]
    in_specs = [ANY] + [vmem] * (1 + len(kernels))
    if last is not None:
        operands += list(last)
        in_specs += [vmem, ANY, vmem, vmem]
        scratch += [pltpu.VMEM(last[1].shape, BF16)] + [pltpu.VMEM((rows, width), F32)] * 2
    return pl.pallas_call(
        functools.partial(step_kernel, scale, at, each, group, len(kernels), last is not None),
        in_specs=in_specs,
        out_specs=vmem,
        out_shape=jax.ShapeDtypeStruct((rows, width), F32 if last is None else BF16),
        scratch_shapes=scratch,
        compiler_params=params(24),
        cost_estimate=cost(4 * count * rows * depth * width, 8 * MIB),
        name="step_part" if last is None else "step_last",
    )(*operands)


def last_kernel(each, order, trial, *refs):
    *blocks, out, held, sems = refs
    copies = [
        pltpu.make_async_copy(block, held.at[order[r]], sems.at[r])
        for r, block in enumerate(blocks)
    ]

    @pl.when(pl.program_id(0) == 0)
    def _():
        for copy in copies:
            copy.start()
        for copy in copies:
            copy.wait()

    width, columns = held.shape[2], trial.shape[1]
    points = trial.shape[0] // width
    size = points * each
    here = pl.ds(pl.multiple_of(pl.program_id(0) * size, size), size)
    part = held[:, here, :].astype(F32).reshape(len(blocks), points, each, width)
    for p in range(points):
        rows = part[:, p].reshape(columns, width)
        at = slice(p * width, (p + 1) * width)
        out[at] = 2.0 * rows.T - trial[at].astype(F32)


def last_call(blocks, order, trial, each, points):
    total, columns = trial.shape
    rows, width = blocks[0].shape
    if each % 8 != 0:
        place = jnp.zeros_like(order).at[order].set(jnp.arange(order.shape[0], dtype=jnp.int32))
        held = jnp.stack(blocks)[place].reshape(len(blocks), -1, each, width)
        summed = jnp.transpose(held, (1, 3, 0, 2)).reshape(total, columns)
        return 2.0 * summed.astype(F32) - trial.astype(F32)
    step = 8 * width
    row_block = pl.BlockSpec((step, columns), lambda s, o: (s, 0))
    return pl.pallas_call(
        functools.partial(last_kernel, each),
        grid_spec=pltpu.PrefetchScalarGridSpec(
            num_scalar_prefetch=1,
            grid=(total // step,),
            in_specs=[row_block] + [ANY] * len(blocks),
            out_specs=row_block,
            scratch_shapes=[
                pltpu.VMEM((len(blocks), rows, width), BF16),
                pltpu.SemaphoreType.DMA((len(blocks),)),
            ],
        ),
        out_shape=jax.ShapeDtypeStruct((total, columns), F32),
        compiler_params=params(24),
        cost_estimate=cost(2 * total * columns * width, 8 * MIB),
        name="last_call",
    )(order, trial, *blocks)


def shards(screened, density, transform, energy, trial, coarse_index, interp_weight, bands):
    pair_count = lax.axis_size("pair")
    plane_count = lax.axis_size("pw")
    row_index = lax.axis_index("pair")
    col_index = lax.axis_index("pw")
    transitions = density.shape[2]
    row_points, col_points, neighbours = coarse_index.shape
    fine_points = bands.shape[0]
    columns = trial.shape[1]
    each = columns // pair_count
    norm_scale = 1.0 / math.sqrt(fine_points * transitions)
    order = pair_order()

    density_blocks = plane_blocks(density[0])

    table = jnp.concatenate([coarse_index.astype(BF16), interp_weight], axis=2)
    table, rows_from = small_pair_blocks(table.reshape(row_points, -1))
    table = table.reshape(pair_count, -1)
    first_pair = (col_index * pair_count) // plane_count
    wanted = (jnp.arange(pair_count) + first_pair) % pair_count
    sort = (wanted[:, None] == rows_from[None, :]).astype(BF16)
    table = dot(sort, table).reshape(fine_points, col_points, -1)
    names = order.astype(F32)

    def coefficients(index, weight):
        hit = index.astype(F32)[..., None, :] == names[:, None]
        return jnp.sum(jnp.where(hit, weight.astype(F32)[..., None, :], 0.0), axis=-1)

    mix = coefficients(table[..., :neighbours], table[..., neighbours:])
    mix = jnp.transpose(mix, (2, 1, 0)).astype(BF16)
    row_mix = coefficients(coarse_index, interp_weight)
    row_mix = jnp.transpose(row_mix, (2, 0, 1)).astype(BF16)

    positions = jnp.arange(transitions) % NCOND
    live = (positions[None, :] < bands[:, None]).astype(F32)
    my_live = lax.dynamic_slice_in_dim(live, col_index * col_points, col_points, 0)
    energies = energy.reshape(col_points, transitions)
    pick = (
        jnp.arange(columns)[None, :] == row_index * each + jnp.arange(each)[:, None]
    ).astype(BF16)

    start, my_start, my_trial = start_call(pick, transform, trial, my_live)
    start_blocks = plane_blocks(my_start)

    planes = jnp.stack([(col_index + d) % plane_count for d in range(plane_count)])
    planes = planes.astype(jnp.int32)
    left, own = left_product(planes[:1], screened, density[0])
    packed = coarse_block(planes[1:], left, own, density_blocks[1:])

    folded, shift = fold_call(transform, my_live, energies, my_trial, norm_scale, each, packed)
    mixer, mixed = mix_all(mix, start_blocks, each, packed)
    row_mixed = row_mix_all(row_mix, start, packed)
    row_mixed = row_mixed.reshape(pair_count, row_points * columns, transitions)
    first_point = row_index * row_points
    wanted = lax.dynamic_slice_in_dim(transform, first_point % col_points, row_points, 0)
    wanted, _ = lax.optimization_barrier((wanted, packed))
    wanted_blocks = plane_blocks(wanted)
    root = first_point // col_points
    row_transform = wanted
    for step in range(1, plane_count):
        from_root = (col_index + step) % plane_count == root
        row_transform = jnp.where(from_root, wanted_blocks[step], row_transform)

    blocks = pair_blocks(plane_sum(packed).astype(BF16))
    early = len(pair_moves()[0])
    kernels_early, total = through(mixed, 0, blocks[:early], each)
    kernels_late, total, again = through(mixed, early, blocks[early:], each, total, folded, shift)
    kernels = [kernels_early, kernels_late]
    again_blocks = plane_blocks(again)
    energy_part = energy_call(
        transform, total, my_live, energies, my_trial, norm_scale, each, again
    )

    back = jnp.zeros(again.shape, F32)
    if again.shape[0] % 128 != 0:
        again_blocks = [jnp.concatenate(again_blocks, axis=0)]
    for step in range(len(again_blocks) - 1):
        part = step_call(mixer, again_blocks[step], step, kernels, norm_scale, each)
        back = part if step == 0 else back + part
    second = step_call(
        mixer, again_blocks[-1], len(again_blocks) - 1, kernels, norm_scale, each,
        (back, transform, my_live, energy_part),
    )
    second_blocks = pair_blocks(second)

    row_back = row_through(row_mixed, kernels, second)
    row_back = row_back.reshape(row_points, columns, transitions)
    row_part = jnp.einsum("ksv,kns->kvn", row_transform, row_back, preferred_element_type=F32)
    row_live = lax.dynamic_slice_in_dim(live, first_point, row_points, 0)
    row_energy = lax.dynamic_slice_in_dim(energies, first_point % col_points, row_points, 0)
    trial_blocks = trial.reshape(col_points, transitions, columns)
    row_trial = lax.dynamic_slice_in_dim(trial_blocks, first_point % col_points, row_points, 0)
    diagonal = jnp.where(root == col_index, row_energy[:, :, None] * row_trial.astype(F32), 0.0)
    row_part = row_part * norm_scale * row_live[:, :, None] + diagonal
    first_step = plane_sum(row_part.astype(BF16)).astype(BF16)
    first_step = first_step.reshape(row_points * transitions, columns)

    second_step = last_call(second_blocks, order.astype(jnp.int32), trial, each, col_points)
    return (first_step, second_step)


def solution(mesh):
    in_specs = (
        P("pair", "pw", None),
        P("pair", "pw", None),
        P("pw", None, None),
        P("pw"),
        P("pw", None),
        P("pair", "pw", None),
        P("pair", "pw", None),
        P(),
    )
    out_specs = (P("pair", None), P("pw", None))
    return jax.shard_map(shards, mesh=mesh, in_specs=in_specs, out_specs=out_specs, check_vma=False)
```

```python
import functools
import math

import jax
import jax.numpy as jnp
from jax import lax
from jax.experimental import pallas as pl
from jax.experimental.pallas import tpu as pltpu
from jax.sharding import PartitionSpec as P

NCOND = 16
F32 = jnp.float32
BF16 = jnp.bfloat16
MIB = 1 << 20
NN = (((1,), (0,)), ((), ()))
NT = (((1,), (1,)), ((), ()))
TN = (((0,), (0,)), ((), ()))


def dot(a, b, dims=NN):
    return lax.dot_general(a, b, dims, preferred_element_type=F32)


def cost(flops, read):
    return pl.CostEstimate(flops=1, bytes_accessed=1, transcendentals=0)


def params(mib):
    return pltpu.CompilerParams(vmem_limit_bytes=mib * MIB)


def whole(shape):
    return pl.BlockSpec(shape, lambda *_: (0,) * len(shape))


ANY = pl.BlockSpec(memory_space=pl.ANY)
HBM = pl.BlockSpec(memory_space=pltpu.HBM)
VMEM = pl.BlockSpec(memory_space=pltpu.VMEM)
SMEM = pl.BlockSpec(memory_space=pltpu.SMEM)


def far(value):
    return pltpu.with_memory_space_constraint(value, pltpu.HBM)


def shaped(shape, dtype=BF16):
    return jax.ShapeDtypeStruct(shape, dtype)


def far_shaped(shape):
    return pltpu.HBM(shape, BF16)


def loads(source, target, sems, pieces, axis=0, first=0):
    size = target.shape[axis] // pieces
    copies = []
    for p in range(pieces):
        at = (slice(None),) * axis + (pl.ds(p * size, size),)
        copies.append(pltpu.make_async_copy(source.at[at], target.at[at], sems.at[first + p]))
        copies[-1].start()
    return copies


def store(source, target, at, sem, copies):
    copies.append(pltpu.make_async_copy(source.at[at], target.at[at], sem))
    copies[-1].start()


def finish(copies):
    for copy in copies:
        copy.wait()


def from_ahead(value, axis, step):
    count = lax.axis_size(axis)
    return lax.ppermute(value, axis, [((s + step) % count, s) for s in range(count)])


def flipped(value, axis, bit):
    count = lax.axis_size(axis)
    return lax.ppermute(value, axis, [(s, s ^ bit) for s in range(count)])


def plane_blocks(value):
    return [value] + [from_ahead(value, "pw", d) for d in range(1, lax.axis_size("pw"))]


def pair_moves():
    groups = lax.axis_size("pair") // 4
    far = sorted(range(groups), key=lambda d: min(d, groups - d))
    early = [(d, 0, 0) for d in far] + [(0, 1, 0)] + [(d, 0, 1) for d in far] + [(0, 1, 1)]
    early += [(d, 1, 0) for d in far[1:-1]]
    late = [(d, 1, 1) for d in far[1:-1]] + [(far[-1], 1, 0), (far[-1], 1, 1)]
    return early, late


def after(value, *others):
    return lax.optimization_barrier((value, *others))[0]


def pair_blocks(value, meanwhile=None):
    early, late = pair_moves()
    far_moves = [move for move in early if move[0] and not move[1] and not move[2]]
    held = {(0, 0, 0): value, (0, 1, 0): flipped(value, "pair", 2)}
    for move in far_moves:
        ready = value
        if meanwhile is None and move == far_moves[-1]:
            ready = after(value, *[held[other] for other in far_moves[:-1]])
        held[move] = from_ahead(ready, "pair", 4 * move[0])
    done = None
    if meanwhile is not None:
        held[0, 0, 1] = flipped(value, "pair", 1)
        done = meanwhile(held[0, 0, 1])
        for move in far_moves:
            held[move] = after(held[move], done)
    for move in early + late:
        far, side, core = move
        if core and move not in held:
            held[move] = flipped(held[far, side, 0], "pair", 1)
        elif side and far and not core:
            held[move] = flipped(held[far, 0, 0], "pair", 2)
    return [held[move] for move in early + late], done


def pair_order():
    early, late = pair_moves()
    me = lax.axis_index("pair")
    count = lax.axis_size("pair")
    return jnp.stack([((me + 4 * far) % count) ^ (2 * side + core) for far, side, core in early + late])


def small_pair_blocks(value, names):
    count = lax.axis_size("pair")
    steps = range(1, count // 4)
    value = jnp.concatenate([value] + [from_ahead(value, "pair", 4 * d) for d in steps])
    me = lax.axis_index("pair")
    index = jnp.stack([(me + 4 * d) % count for d in range(count // 4)])
    value = jnp.concatenate([value] + [flipped(value, "pair", bits) for bits in (2, 1, 3)])
    index = jnp.concatenate([index ^ bits for bits in (0, 2, 1, 3)])
    return value, names[index].reshape(-1)


def plane_sum(value):
    blocks = plane_blocks(value)
    if len(blocks) == 2:
        return blocks[0].astype(F32) + blocks[1].astype(F32)
    stacked = jnp.roll(jnp.stack(blocks), lax.axis_index("pw"), axis=0)
    return jnp.sum(stacked.astype(F32), axis=0)


def iotas(rows, cols):
    return (
        lax.broadcasted_iota(jnp.int32, (rows, cols), 0),
        lax.broadcasted_iota(jnp.int32, (rows, cols), 1),
    )


def pack(symmetric, out):
    half = symmetric.shape[0] // 2
    row, col = iotas(half, half)
    upper, lower = symmetric[:half, :half], symmetric[half:, half:]
    diagonal = jnp.sum(jnp.where(row == col, upper, 0.0), axis=0, keepdims=True)
    out[:half] = symmetric[:half, half:].astype(BF16)
    out[half : 2 * half] = jnp.where(row > col, upper, lower).astype(BF16)
    out[2 * half :] = jnp.broadcast_to(diagonal, (16, half)).astype(BF16)


def unpack(packed):
    half = packed.shape[1]
    row, col = iotas(half, half)
    corner = packed[:half]
    both = packed[half : 2 * half].astype(F32)
    diagonal = packed[2 * half : 2 * half + 1].astype(F32)
    other = both.T
    upper = jnp.where(row > col, both, jnp.where(row == col, diagonal, other))
    lower = jnp.where(row <= col, both, other)
    top = jnp.concatenate([upper.astype(BF16), corner], axis=1)
    bottom = jnp.concatenate([corner.T, lower.astype(BF16)], axis=1)
    return jnp.concatenate([top, bottom], axis=0)


def left_kernel(plane, screened_at, density, _, out_at, total, screened, turned, out, sems):
    pieces = sems.shape[0] // 2
    copies = loads(screened_at.at[0], screened, sems, pieces, axis=1)
    stores = []
    rows = density.shape[0]
    turned[...] = density[...].T
    size = out.shape[1] // pieces
    for p in range(pieces):
        copies[p].wait()
        at = slice(p * size, (p + 1) * size)
        out[:, at] = dot(turned[...], screened[:, at]).astype(BF16)
        at = (slice(None), pl.ds(p * size, size))
        store(out, out_at, at, sems.at[pieces + p], stores)
    at = pl.multiple_of(plane[0] * rows, rows)
    total[...] = dot(out[:, pl.ds(at, rows)], density[...])
    finish(stores)


def left_product(plane, screened, density, later):
    rows, width = density.shape
    depth = screened.shape[2]
    return pl.pallas_call(
        left_kernel,
        in_specs=[SMEM, HBM, VMEM, ANY],
        out_specs=[HBM, VMEM],
        out_shape=[far_shaped((width, depth)), shaped((width, width), F32)],
        scratch_shapes=[
            pltpu.VMEM((rows, depth), BF16),
            pltpu.VMEM((width, rows), BF16),
            pltpu.VMEM((width, depth), BF16),
            pltpu.SemaphoreType.DMA((16,)),
        ],
        compiler_params=params(24),
        cost_estimate=cost(2 * rows * depth * width, 2 * rows * depth),
        name="left_product",
    )(plane, far(screened), density, later)


def coarse_kernel(planes, left_at, total, *refs):
    *blocks, _, _, out, left, sems = refs
    copies = []
    for step, block in enumerate(blocks):
        rows = block.shape[0]
        at = pl.multiple_of(planes[step] * rows, rows)
        part = left_at.at[:, pl.ds(at, rows)]
        copies.append(pltpu.make_async_copy(part, left.at[step], sems.at[step]))
        copies[-1].start()
    raw = total[...]
    for step, block in enumerate(blocks):
        copies[step].wait()
        raw = raw + dot(left[step], block[...])
    pack(0.5 * (raw + raw.T), out)


def coarse_block(planes, left, total, density_blocks, later):
    width = left.shape[0]
    return pl.pallas_call(
        coarse_kernel,
        in_specs=[SMEM, HBM] + [VMEM] * (1 + len(density_blocks)) + [ANY] * 2,
        out_specs=VMEM,
        out_shape=shaped((width + 16, width // 2)),
        scratch_shapes=[
            pltpu.VMEM((len(density_blocks), width, density_blocks[0].shape[0]), BF16),
            pltpu.SemaphoreType.DMA((len(density_blocks),)),
        ],
        compiler_params=params(16),
        cost_estimate=cost(width * width * left.shape[1], 4 * MIB),
        name="coarse_block",
    )(planes, far(left), total, *density_blocks, *later)


def spread(table, each, same):
    rows, cols = table.shape
    tall = jnp.broadcast_to(table[:, None, :], (rows, each, cols)).reshape(rows * each, cols)
    return (tall * same).astype(BF16)


def same_column(rows, cols, each):
    row, col = iotas(rows, cols)
    return jnp.where(((row ^ col) & (each - 1)) == 0, 1.0, 0.0)


def widening(names, cols, each):
    col = lax.broadcasted_iota(jnp.int32, (names.shape[0], cols), 1)
    return jnp.where((col >= names * each) & (col < (names + 1) * each), 1.0, 0.0).astype(BF16)


def mix_kernel(each, points, order, table, names, *refs):
    *blocks, mixer_at, mixed, wide, same, mixer, sems = refs
    count, rows, cols = mixer.shape
    stores = []
    same[...] = same_column(rows, cols, each)
    chunks = wide.shape[0] // table.shape[1]
    row = lax.broadcasted_iota(jnp.int32, names.shape, 0)
    for p in range(chunks):
        here = jnp.where(row % chunks == p, names[...], -1)
        at = slice(p * table.shape[1], (p + 1) * table.shape[1])
        wide[at] = dot(table[...], widening(here, cols, each), TN)
    for c in range(count):
        at = pl.multiple_of(order[c] * points, points)
        part = spread(wide[pl.ds(at, points), :], each, same[...])
        mixer[c] = part
        total, at = 0.0, 0
        for block in blocks:
            depth = block.shape[0]
            total = total + dot(part[:, at : at + depth], block[...])
            at += depth
        mixed[c] = total.astype(BF16)
        if c % 2 == 1:
            store(mixer, mixer_at, pl.ds(c - 1, 2), sems.at[c // 2], stores)
    finish(stores)


def mix_all(order, table, names, blocks, points, each):
    count = order.shape[0]
    cols = sum(block.shape[0] for block in blocks)
    width = blocks[0].shape[1]
    mixer = (count, points * each, cols)
    mixed = (count, points * each, width)
    return pl.pallas_call(
        functools.partial(mix_kernel, each, points),
        in_specs=[SMEM, VMEM, VMEM] + [VMEM] * len(blocks),
        out_specs=[HBM, VMEM],
        out_shape=[far_shaped(mixer), shaped(mixed)],
        scratch_shapes=[
            pltpu.VMEM((count * points, cols), F32),
            pltpu.VMEM(mixer[1:], F32),
            pltpu.VMEM(mixer, BF16),
            pltpu.SemaphoreType.DMA((count // 2,)),
        ],
        compiler_params=params(16),
        cost_estimate=cost(4 * count * points * cols * each * width, 8 * MIB),
        name="mix_all",
    )(order, table, names, *blocks)


def row_kernel(each, parts, order, table, vectors_at, *refs):
    kernels, refs = refs[:parts], refs[parts:]
    _, out, vectors, mixed, sems = refs
    points, columns, width = vectors.shape
    count, rows = mixed.shape[:2]
    pieces = sems.shape[0]
    group = columns // pieces
    copies = loads(vectors_at, vectors, sems, pieces, axis=1)
    names = lax.broadcasted_iota(jnp.int32, (points, 1), 0)
    cols = points * each
    wide = dot(table[...], widening(names, cols, each))
    mixer = spread(wide, each, same_column(count * rows * each, cols, each))
    for p in range(pieces):
        copies[p].wait()
        at = slice(p * group, (p + 1) * group)
        value = vectors[:, at, :].astype(F32).reshape(points, group // each, each, width)
        parts = []
        for g in range(group // each):
            flat = value[:, g].reshape(cols, width).astype(BF16)
            parts.append(dot(mixer, flat).reshape(count * rows, each, width))
        joined = jnp.concatenate(parts, axis=1).astype(BF16)
        mixed[:, :, at, :] = joined.reshape(count, rows, group, width)
    total, c = 0.0, 0
    for kernel in kernels:
        for k in range(kernel.shape[0]):
            total = total + dot(mixed[order[c]].reshape(out.shape), kernel[k])
            c += 1
    out[...] = total.astype(BF16)


def row_call(order, mix, vectors, kernels, later):
    count, rows, points = mix.shape
    columns, width = vectors.shape[1:]
    each = 8
    return pl.pallas_call(
        functools.partial(row_kernel, each, len(kernels)),
        in_specs=[SMEM, VMEM, HBM] + [VMEM] * len(kernels) + [ANY],
        out_specs=VMEM,
        out_shape=shaped((rows * columns, width)),
        scratch_shapes=[
            pltpu.VMEM(vectors.shape, BF16),
            pltpu.VMEM((count, rows, columns, width), BF16),
            pltpu.SemaphoreType.DMA((columns // (2 * each),)),
        ],
        compiler_params=params(24),
        cost_estimate=cost(1, 1),
        name="row_call",
    )(order, mix.reshape(count * rows, points), far(vectors), *kernels, later)


def start_kernel(each, index, pick, transform_at, trial_at, live, table, *refs):
    start_at, mine, my_trial, table_out, transform, trial, start, held, rows, sems = refs
    pieces = 4
    load_trial = loads(trial_at, trial, sems, pieces)
    load_transform = loads(transform_at, transform, sems, pieces, first=pieces)
    table_out[...] = table[...]
    points, width, _ = transform.shape
    group = points // pieces
    at_mine = pl.ds(pl.multiple_of(index[0] * each, each), each)
    stores = []
    for p in range(pieces):
        load_trial[p].wait()
        load_transform[p].wait()
        for k in range(p * group, (p + 1) * group):
            here = slice(k * each, (k + 1) * each)
            block = trial[k * width : (k + 1) * width, :]
            turned_block = block.astype(F32).T
            vectors = turned_block * live[k : k + 1, :]
            turned = dot(vectors.astype(BF16), transform[k], NT)
            start[k] = turned.astype(BF16)
            if each % 8 == 0:
                rows[0] = turned_block
                rows[1] = turned
                my_trial[here] = rows[0, at_mine, :]
                held[here] = rows[1, at_mine, :]
            else:
                my_trial[here] = dot(pick[...], block, NT)
                held[here] = dot(pick[...], start[k])
        store(start, start_at, pl.ds(p * group, group), sems.at[2 * pieces + p], stores)
    mine[...] = held[...].astype(BF16)
    finish(stores)


def start_call(index, pick, transform, trial, live, table):
    each, columns = pick.shape
    points, width, _ = transform.shape
    mine = (points * each, width)
    return pl.pallas_call(
        functools.partial(start_kernel, each),
        in_specs=[SMEM, VMEM, HBM, HBM, VMEM, VMEM],
        out_specs=[HBM] + [VMEM] * 3,
        out_shape=[
            far_shaped((points, columns, width)),
            shaped(mine),
            shaped(mine, F32),
            shaped(table.shape),
        ],
        scratch_shapes=[
            pltpu.VMEM(transform.shape, BF16),
            pltpu.VMEM(trial.shape, BF16),
            pltpu.VMEM((points, columns, width), BF16),
            pltpu.VMEM(mine, F32),
            pltpu.VMEM((2, columns, width), F32),
            pltpu.SemaphoreType.DMA((12,)),
        ],
        compiler_params=params(16),
        cost_estimate=cost(4 * points * columns * width * width, 8 * MIB),
        name="start_call",
    )(index, pick, far(transform), far(trial), live, table)


def fold_kernel(scale, each, place, transform_at, live, energy, my_trial, *refs):
    folded_at, shift, wanted_at, transform, folded, sems = refs
    pieces = 4
    group = transform.shape[0] // pieces
    copies = loads(transform_at, transform, sems, pieces)
    stores = []
    for p in range(pieces):
        copies[p].wait()
        for k in range(p * group, (p + 1) * group):
            here = slice(k * each, (k + 1) * each)
            table = transform[k]
            masked = (table.astype(F32) * (scale * live[k : k + 1, :])).astype(BF16)
            folded[k] = dot(masked, table, NT).astype(BF16)
            vectors = my_trial[here] * (live[k : k + 1, :] * energy[k : k + 1, :])
            shift[here] = dot(vectors.astype(BF16), table, NT)
        store(folded, folded_at, pl.ds(p * group, group), sems.at[pieces + p], stores)
    wanted = transform.at[pl.ds(place[0], wanted_at.shape[0])]
    stores.append(pltpu.make_async_copy(wanted, wanted_at, sems.at[2 * pieces]))
    stores[-1].start()
    finish(stores)


def fold_call(place, rows, transform, live, energy, my_trial, scale, each):
    points, width, _ = transform.shape
    vectors = (points * each, width)
    return pl.pallas_call(
        functools.partial(fold_kernel, scale, each),
        in_specs=[SMEM, HBM] + [VMEM] * 3,
        out_specs=[HBM, VMEM, HBM],
        out_shape=[
            far_shaped(transform.shape),
            shaped(vectors, F32),
            far_shaped((rows, width, width)),
        ],
        scratch_shapes=[
            pltpu.VMEM(transform.shape, BF16),
            pltpu.VMEM(transform.shape, BF16),
            pltpu.SemaphoreType.DMA((9,)),
        ],
        compiler_params=params(16),
        cost_estimate=cost(3 * points * width * width * width, 8 * MIB),
        name="fold_call",
    )(place, far(transform), live, energy, my_trial)


def by_point(each, points, body, store):
    step = max(each, 8)
    group = step // each
    owner = lax.broadcasted_iota(jnp.int32, (step, 1), 0) // each
    for b in range(points // group):
        here = slice(b * step, (b + 1) * step)
        if group == 1:
            value = body(here, b)
        else:
            value = 0.0
            for p in range(group):
                value = value + jnp.where(owner == p, body(here, b * group + p), 0.0)
        store[here] = value


def through_kernel(first, count, each, last, mixed, *refs):
    packed, refs = refs[:count], refs[count:]
    if last:
        before, folded_at, shift, kernels, total, again, folded, held, sem = refs
        load_folded = pltpu.make_async_copy(folded_at, folded, sem)
        load_folded.start()
    else:
        kernels, total = refs
    value = before[...] if last else 0.0
    for c in range(count):
        kernels[c] = unpack(packed[c][...])
        value = value + dot(mixed[first + c], kernels[c])
    total[...] = value
    if last:
        load_folded.wait()

        def body(here, k):
            return dot(total[here].astype(BF16), folded[k]) + shift[here]

        by_point(each, folded.shape[0], body, held)
        again[...] = held[...].astype(BF16)


def through(mixed, first, packed, each, before=None, folded=None, shift=None):
    _, rows, width = mixed.shape
    count = len(packed)
    last = before is not None
    out_shape = [shaped((count, width, width)), shaped((rows, width), F32)]
    scratch = []
    operands = [mixed, *packed]
    in_specs = [VMEM] * (1 + count)
    if last:
        out_shape.append(shaped((rows, width)))
        scratch = [
            pltpu.VMEM(folded.shape, BF16),
            pltpu.VMEM((rows, width), F32),
            pltpu.SemaphoreType.DMA,
        ]
        operands += [before, far(folded), shift]
        in_specs += [VMEM, HBM, VMEM]
    return pl.pallas_call(
        functools.partial(through_kernel, first, count, each, last),
        in_specs=in_specs,
        out_specs=[VMEM] * len(out_shape),
        out_shape=out_shape,
        scratch_shapes=scratch,
        compiler_params=params(24),
        cost_estimate=cost(8 * count * rows * width * width, 8 * MIB),
        name="through_last" if last else "through_early",
    )(*operands)


def mix_and_through(mixer_at, mixer, vectors, at, kernel_refs, sems, next_load):
    depth = vectors.shape[0]
    pieces = sems.shape[0]
    columns = mixer_at.at[:, :, pl.ds(at, depth)]
    copies = loads(columns, mixer, sems, pieces)
    next_load.start()
    group = mixer.shape[0] // pieces
    value, c = 0.0, 0
    for ref in kernel_refs:
        for k in range(ref.shape[0]):
            if c % group == 0:
                copies[c // group].wait()
            mixed = dot(mixer[c], vectors[...]).astype(BF16)
            value = value + dot(mixed, ref[k])
            c += 1
    return value


def step_part_kernel(scale, each, parts, mixer_at, vectors, *refs):
    kernels, refs = refs[:parts], refs[parts:]
    transform_at, total, live, energy, trial, out, shift, mixer, transform, sems, sem = refs
    load = pltpu.make_async_copy(transform_at, transform, sem)
    out[...] = mix_and_through(mixer_at, mixer, vectors, 0, kernels, sems, load)
    load.wait()

    def body(here, k):
        turned = dot(total[here].astype(BF16), transform[k])
        row = energy[k : k + 1, :]
        return (turned * (scale * live[k : k + 1, :]) + row * trial[here]) * row

    by_point(each, transform.shape[0], body, shift)


def step_part(mixer, vectors, kernels, transform, total, live, energy, my_trial, scale, each):
    rows, width = total.shape
    operands = [far(mixer), vectors, *kernels, far(transform), total, live, energy, my_trial]
    return pl.pallas_call(
        functools.partial(step_part_kernel, scale, each, len(kernels)),
        in_specs=[HBM] + [VMEM] * (1 + len(kernels)) + [HBM] + [VMEM] * 4,
        out_specs=[VMEM, VMEM],
        out_shape=[shaped((rows, width), F32)] * 2,
        scratch_shapes=[
            pltpu.VMEM((mixer.shape[0], rows, vectors.shape[0]), BF16),
            pltpu.VMEM(transform.shape, BF16),
            pltpu.SemaphoreType.DMA((4,)),
            pltpu.SemaphoreType.DMA,
        ],
        compiler_params=params(24),
        cost_estimate=cost(1, 1),
        name="step_part",
    )(*operands)


def step_last_kernel(scale, at, each, parts, mixer_at, vectors, *refs):
    kernels, refs = refs[:parts], refs[parts:]
    before, transform_at, live, shift, out, total, held, mixer, transform, sems, sem = refs
    load = pltpu.make_async_copy(transform_at, transform, sem)
    value = mix_and_through(mixer_at, mixer, vectors, at, kernels, sems, load)
    total[...] = before[...] + value
    load.wait()

    def body(here, k):
        turned = dot(total[here].astype(BF16), transform[k])
        return turned * (scale * live[k : k + 1, :]) + shift[here]

    by_point(each, transform.shape[0], body, held)
    out[...] = held[...].astype(BF16)


def step_last(mixer, vectors, at, kernels, before, transform, live, shift, scale, each):
    rows, width = before.shape
    operands = [far(mixer), vectors, *kernels, before, far(transform), live, shift]
    return pl.pallas_call(
        functools.partial(step_last_kernel, scale, at, each, len(kernels)),
        in_specs=[HBM] + [VMEM] * (2 + len(kernels)) + [HBM, VMEM, VMEM],
        out_specs=VMEM,
        out_shape=shaped((rows, width)),
        scratch_shapes=[
            pltpu.VMEM((rows, width), F32),
            pltpu.VMEM((rows, width), F32),
            pltpu.VMEM((mixer.shape[0], rows, vectors.shape[0]), BF16),
            pltpu.VMEM(transform.shape, BF16),
            pltpu.SemaphoreType.DMA((4,)),
            pltpu.SemaphoreType.DMA,
        ],
        compiler_params=params(24),
        cost_estimate=cost(1, 1),
        name="step_last",
    )(*operands)


def last_kernel(each, order, trial_at, *refs):
    *blocks, out_at, held, trial, out, in_sems, out_sems, sems = refs
    pieces = out_sems.shape[0]
    copies = [
        pltpu.make_async_copy(block, held.at[order[r]], sems.at[r])
        for r, block in enumerate(blocks)
    ]
    for copy in copies:
        copy.start()
    load_trial = loads(trial_at, trial, in_sems, pieces)
    finish(copies)
    width, columns = held.shape[2], trial.shape[1]
    points = trial.shape[0] // width // pieces
    stores = []
    for p in range(pieces):
        load_trial[p].wait()
        part = held[:, p * points * each : (p + 1) * points * each, :].astype(F32)
        part = part.reshape(len(blocks), points, each, width)
        for k in range(points):
            rows = part[:, k].reshape(columns, width)
            first = (p * points + k) * width
            at = slice(first, first + width)
            out[at] = 2.0 * rows.T - trial[at].astype(F32)
        at = pl.ds(p * points * width, points * width)
        store(out, out_at, at, out_sems.at[p], stores)
    finish(stores)


def last_call(blocks, order, trial, each):
    total, columns = trial.shape
    rows, width = blocks[0].shape
    if each % 8 != 0:
        place = jnp.zeros_like(order).at[order].set(jnp.arange(order.shape[0], dtype=jnp.int32))
        held = jnp.stack(blocks)[place].reshape(len(blocks), -1, each, width)
        summed = jnp.transpose(held, (1, 3, 0, 2)).reshape(total, columns)
        return 2.0 * summed.astype(F32) - trial.astype(F32)
    pieces = 8
    return pl.pallas_call(
        functools.partial(last_kernel, each),
        in_specs=[SMEM, HBM] + [ANY] * len(blocks),
        out_specs=HBM,
        out_shape=shaped((total, columns), F32),
        scratch_shapes=[
            pltpu.VMEM((len(blocks), rows, width), BF16),
            pltpu.VMEM((total, columns), BF16),
            pltpu.VMEM((total, columns), F32),
            pltpu.SemaphoreType.DMA((pieces,)),
            pltpu.SemaphoreType.DMA((pieces,)),
            pltpu.SemaphoreType.DMA((len(blocks),)),
        ],
        compiler_params=params(24),
        cost_estimate=cost(2 * total * columns * width, 8 * MIB),
        name="last_call",
    )(order, far(trial), *blocks)


def shards(screened, density, transform, energy, trial, coarse_index, interp_weight, bands):
    pair_count = lax.axis_size("pair")
    plane_count = lax.axis_size("pw")
    row_index = lax.axis_index("pair")
    col_index = lax.axis_index("pw")
    transitions = density.shape[2]
    row_points, col_points, neighbours = coarse_index.shape
    fine_points = bands.shape[0]
    columns = trial.shape[1]
    each = columns // pair_count
    norm_scale = 1.0 / math.sqrt(fine_points * transitions)
    order = pair_order().astype(jnp.int32)

    density_blocks = plane_blocks(density[0])

    names = jnp.arange(pair_count, dtype=jnp.int32)
    hit = jnp.swapaxes(coarse_index, 1, 2)[:, None, :, :] == names[None, :, None, None]
    weight = jnp.swapaxes(interp_weight, 1, 2).astype(F32)[:, None, :, :]
    dense = jnp.sum(jnp.where(hit, weight, 0.0), axis=2).astype(BF16)

    positions = jnp.arange(transitions) % NCOND
    live = (positions[None, :] < bands[:, None]).astype(F32)
    my_live = lax.dynamic_slice_in_dim(live, col_index * col_points, col_points, 0)
    energies = energy.reshape(col_points, transitions)
    pick = (
        jnp.arange(columns)[None, :] == row_index * each + jnp.arange(each)[:, None]
    ).astype(BF16)

    table = dense.reshape(row_points, -1)
    chunks = table.shape[1] // 128
    start, my_start, my_trial, table = start_call(
        row_index[None].astype(jnp.int32), pick, transform, trial, my_live,
        table.reshape(row_points * chunks, 128),
    )

    points_of = jnp.arange(fine_points, dtype=jnp.int32).reshape(pair_count, row_points)
    points_of = (points_of - col_index * col_points) % fine_points
    points_of = jnp.repeat(points_of, chunks, axis=1)
    table, rows_from = small_pair_blocks(after(table, density_blocks[-1]), points_of)
    rows_from = rows_from[:, None]

    planes = jnp.stack([(col_index + d) % plane_count for d in range(plane_count)])
    planes = planes.astype(jnp.int32)
    first_point = row_index * row_points
    place = (first_point % col_points).astype(jnp.int32)
    left, own = left_product(planes[:1], screened, density[0], my_start)
    folded, shift, wanted = fold_call(
        place[None], row_points, transform, my_live, energies, my_trial, norm_scale, each
    )
    packed = coarse_block(planes[1:], left, own, density_blocks[1:], (shift, my_start))
    packed = plane_sum(packed).astype(BF16)

    start_blocks = plane_blocks(after(my_start, packed))
    blocks, _ = pair_blocks(packed)
    side_block = blocks[pair_moves()[0].index((1, 1, 0))]
    mixer, mixed = mix_all(
        order, after(table, side_block), rows_from, start_blocks, col_points, each
    )
    early = len(pair_moves()[0])
    kernels_early, total = through(mixed, 0, blocks[:early], each)
    kernels_late, total, again = through(mixed, early, blocks[early:], each, total, folded, shift)
    kernels = [kernels_early, kernels_late]
    again_blocks = plane_blocks(again)

    near_count = 1
    while near_count * again.shape[0] % 128 != 0:
        near_count += 1
    first_again = jnp.concatenate(again_blocks[:near_count], axis=0)
    other_again = jnp.concatenate(again_blocks[near_count:], axis=0)
    back, shift = step_part(
        mixer, first_again, kernels, transform, total, my_live, energies, my_trial,
        norm_scale, each,
    )
    second = step_last(
        mixer, other_again, first_again.shape[0], kernels, back, transform, my_live, shift,
        norm_scale, each,
    )
    by_point_first = jnp.swapaxes(dense, 0, 1)
    second_blocks, row_back = pair_blocks(
        second, lambda block: row_call(order, by_point_first, start, kernels, block)
    )

    wanted_blocks = plane_blocks(after(wanted, second))
    root = first_point // col_points
    row_transform = wanted
    for step in range(1, plane_count):
        from_root = (col_index + step) % plane_count == root
        row_transform = jnp.where(from_root, wanted_blocks[step], row_transform)
    row_back = row_back.reshape(row_points, columns, transitions)
    row_part = jnp.einsum("ksv,kns->kvn", row_transform, row_back, preferred_element_type=F32)
    row_live = lax.dynamic_slice_in_dim(live, first_point, row_points, 0)
    row_energy = lax.dynamic_slice_in_dim(energies, first_point % col_points, row_points, 0)
    trial_blocks = trial.reshape(col_points, transitions, columns)
    row_trial = lax.dynamic_slice_in_dim(trial_blocks, first_point % col_points, row_points, 0)
    diagonal = jnp.where(root == col_index, row_energy[:, :, None] * row_trial.astype(F32), 0.0)
    row_part = row_part * norm_scale * row_live[:, :, None] + diagonal
    first_step = plane_sum(row_part.astype(BF16)).astype(BF16)
    first_step = first_step.reshape(row_points * transitions, columns)

    second_step = last_call(second_blocks, order, trial, each)
    return (first_step, second_step)


def solution(mesh):
    in_specs = (
        P("pair", "pw", None),
        P("pair", "pw", None),
        P("pw", None, None),
        P("pw"),
        P("pw", None),
        P("pair", "pw", None),
        P("pair", "pw", None),
        P(),
    )
    out_specs = (P("pair", None), P("pw", None))
    return jax.shard_map(shards, mesh=mesh, in_specs=in_specs, out_specs=out_specs, check_vma=False)
```

```python
import functools
import math

import jax
import jax.numpy as jnp
from jax import lax
from jax.experimental import pallas as pl
from jax.experimental.pallas import tpu as pltpu
from jax.sharding import PartitionSpec as P

NCOND = 16
F32 = jnp.float32
BF16 = jnp.bfloat16
MIB = 1 << 20
NN = (((1,), (0,)), ((), ()))
NT = (((1,), (1,)), ((), ()))
TN = (((0,), (0,)), ((), ()))


def dot(a, b, dims=NN):
    return lax.dot_general(a, b, dims, preferred_element_type=F32)


def cost(flops, read):
    return pl.CostEstimate(flops=1, bytes_accessed=1, transcendentals=0)


def params(mib):
    return pltpu.CompilerParams(vmem_limit_bytes=mib * MIB)


def whole(shape):
    return pl.BlockSpec(shape, lambda *_: (0,) * len(shape))


ANY = pl.BlockSpec(memory_space=pl.ANY)
HBM = pl.BlockSpec(memory_space=pltpu.HBM)
VMEM = pl.BlockSpec(memory_space=pltpu.VMEM)
SMEM = pl.BlockSpec(memory_space=pltpu.SMEM)


def far(value):
    return pltpu.with_memory_space_constraint(value, pltpu.HBM)


def shaped(shape, dtype=BF16):
    return jax.ShapeDtypeStruct(shape, dtype)


def far_shaped(shape):
    return pltpu.HBM(shape, BF16)


def loads(source, target, sems, pieces, axis=0, first=0):
    size = target.shape[axis] // pieces
    copies = []
    for p in range(pieces):
        at = (slice(None),) * axis + (pl.ds(p * size, size),)
        copies.append(pltpu.make_async_copy(source.at[at], target.at[at], sems.at[first + p]))
        copies[-1].start()
    return copies


def store(source, target, at, sem, copies):
    copies.append(pltpu.make_async_copy(source.at[at], target.at[at], sem))
    copies[-1].start()


def finish(copies):
    for copy in copies:
        copy.wait()


def from_ahead(value, axis, step):
    count = lax.axis_size(axis)
    return lax.ppermute(value, axis, [((s + step) % count, s) for s in range(count)])


def flipped(value, axis, bit):
    count = lax.axis_size(axis)
    return lax.ppermute(value, axis, [(s, s ^ bit) for s in range(count)])


def plane_blocks(value):
    return [value] + [from_ahead(value, "pw", d) for d in range(1, lax.axis_size("pw"))]


def pair_moves():
    groups = lax.axis_size("pair") // 4
    far = sorted(range(groups), key=lambda d: min(d, groups - d))
    early = [(d, 0, 0) for d in far] + [(0, 1, 0)] + [(d, 0, 1) for d in far] + [(0, 1, 1)]
    early += [(d, 1, 0) for d in far[1:-1]]
    late = [(d, 1, 1) for d in far[1:-1]] + [(far[-1], 1, 0), (far[-1], 1, 1)]
    return early, late


def after(value, *others):
    return lax.optimization_barrier((value, *others))[0]


def pair_blocks(value, meanwhile=None, first=()):
    early, late = pair_moves()
    far_moves = [move for move in early if move[0] and not move[1] and not move[2]]
    held = {(0, 0, 0): value, (0, 1, 0): flipped(value, "pair", 2)}
    for move in far_moves:
        ready = value
        if meanwhile is None and move == far_moves[-1]:
            ready = after(value, *[held[other] for other in far_moves[:-1]], *first)
        held[move] = from_ahead(ready, "pair", 4 * move[0])
    done = None
    if meanwhile is not None:
        done = meanwhile(held[0, 1, 0])
        for move in far_moves:
            held[move] = after(held[move], done)
    for move in early + late:
        far, side, core = move
        if core and move not in held:
            held[move] = flipped(held[far, side, 0], "pair", 1)
        elif side and far and not core:
            held[move] = flipped(held[far, 0, 0], "pair", 2)
    return [held[move] for move in early + late], done


def pair_order():
    early, late = pair_moves()
    me = lax.axis_index("pair")
    count = lax.axis_size("pair")
    return jnp.stack([((me + 4 * far) % count) ^ (2 * side + core) for far, side, core in early + late])


def plane_sum(value):
    blocks = plane_blocks(value)
    if len(blocks) == 2:
        return blocks[0].astype(F32) + blocks[1].astype(F32)
    stacked = jnp.roll(jnp.stack(blocks), lax.axis_index("pw"), axis=0)
    return jnp.sum(stacked.astype(F32), axis=0)


def iotas(rows, cols):
    return (
        lax.broadcasted_iota(jnp.int32, (rows, cols), 0),
        lax.broadcasted_iota(jnp.int32, (rows, cols), 1),
    )


def pack(symmetric, out):
    half = symmetric.shape[0] // 2
    row, col = iotas(half, half)
    upper, lower = symmetric[:half, :half], symmetric[half:, half:]
    diagonal = jnp.sum(jnp.where(row == col, upper, 0.0), axis=0, keepdims=True)
    out[:half] = symmetric[:half, half:].astype(BF16)
    out[half : 2 * half] = jnp.where(row > col, upper, lower).astype(BF16)
    out[2 * half :] = jnp.broadcast_to(diagonal, (16, half)).astype(BF16)


def unpack(packed):
    half = packed.shape[1]
    row, col = iotas(half, half)
    corner = packed[:half]
    both = packed[half : 2 * half].astype(F32)
    diagonal = packed[2 * half : 2 * half + 1].astype(F32)
    other = both.T
    upper = jnp.where(row > col, both, jnp.where(row == col, diagonal, other))
    lower = jnp.where(row <= col, both, other)
    top = jnp.concatenate([upper.astype(BF16), corner], axis=1)
    bottom = jnp.concatenate([corner.T, lower.astype(BF16)], axis=1)
    return jnp.concatenate([top, bottom], axis=0)


def left_kernel(plane, screened_at, density, _, out_at, total, screened, turned, out, sems):
    pieces = sems.shape[0] // 2
    copies = loads(screened_at.at[0], screened, sems, pieces, axis=1)
    stores = []
    rows = density.shape[0]
    turned[...] = density[...].T
    size = out.shape[1] // pieces
    for p in range(pieces):
        copies[p].wait()
        at = slice(p * size, (p + 1) * size)
        out[:, at] = dot(turned[...], screened[:, at]).astype(BF16)
        at = (slice(None), pl.ds(p * size, size))
        store(out, out_at, at, sems.at[pieces + p], stores)
    at = pl.multiple_of(plane[0] * rows, rows)
    total[...] = dot(out[:, pl.ds(at, rows)], density[...])
    finish(stores)


def left_product(plane, screened, density, later):
    rows, width = density.shape
    depth = screened.shape[2]
    return pl.pallas_call(
        left_kernel,
        in_specs=[SMEM, HBM, VMEM, ANY],
        out_specs=[HBM, VMEM],
        out_shape=[far_shaped((width, depth)), shaped((width, width), F32)],
        scratch_shapes=[
            pltpu.VMEM((rows, depth), BF16),
            pltpu.VMEM((width, rows), BF16),
            pltpu.VMEM((width, depth), BF16),
            pltpu.SemaphoreType.DMA((16,)),
        ],
        compiler_params=params(24),
        cost_estimate=cost(2 * rows * depth * width, 2 * rows * depth),
        name="left_product",
    )(plane, far(screened), density, later)


def coarse_kernel(planes, left_at, total, *refs):
    *blocks, _, _, out, left, sems = refs
    copies = []
    for step, block in enumerate(blocks):
        rows = block.shape[0]
        at = pl.multiple_of(planes[step] * rows, rows)
        part = left_at.at[:, pl.ds(at, rows)]
        copies.append(pltpu.make_async_copy(part, left.at[step], sems.at[step]))
        copies[-1].start()
    raw = total[...]
    for step, block in enumerate(blocks):
        copies[step].wait()
        raw = raw + dot(left[step], block[...])
    pack(0.5 * (raw + raw.T), out)


def coarse_block(planes, left, total, density_blocks, later):
    width = left.shape[0]
    return pl.pallas_call(
        coarse_kernel,
        in_specs=[SMEM, HBM] + [VMEM] * (1 + len(density_blocks)) + [ANY] * 2,
        out_specs=VMEM,
        out_shape=shaped((width + 16, width // 2)),
        scratch_shapes=[
            pltpu.VMEM((len(density_blocks), width, density_blocks[0].shape[0]), BF16),
            pltpu.SemaphoreType.DMA((len(density_blocks),)),
        ],
        compiler_params=params(16),
        cost_estimate=cost(width * width * left.shape[1], 4 * MIB),
        name="coarse_block",
    )(planes, far(left), total, *density_blocks, *later)


def spread(table, each, same):
    rows, cols = table.shape
    tall = jnp.broadcast_to(table[:, None, :], (rows, each, cols)).reshape(rows * each, cols)
    return (tall * same).astype(BF16)


def same_column(rows, cols, each):
    row, col = iotas(rows, cols)
    return jnp.where(((row ^ col) & (each - 1)) == 0, 1.0, 0.0)


def widening(names, cols, each):
    col = lax.broadcasted_iota(jnp.int32, (names.shape[0], cols), 1)
    return jnp.where((col >= names * each) & (col < (names + 1) * each), 1.0, 0.0).astype(BF16)


def gathered_weights(order, tables, names, fine, held, out):
    rows = names.shape[0] // len(tables)
    table = jnp.concatenate([ref[ref.shape[0] - rows :, :] for ref in tables], axis=0)
    chunks = out.shape[0] // table.shape[1]
    row = lax.broadcasted_iota(jnp.int32, names.shape, 0)
    col = lax.broadcasted_iota(jnp.int32, (names.shape[0], fine), 1)
    for p in range(chunks):
        here = jnp.where(row % chunks == p, names[...], -1)
        place = jnp.where(col == here, 1.0, 0.0).astype(BF16)
        at = slice(p * table.shape[1], (p + 1) * table.shape[1])
        held[at] = dot(table, place, TN)
    points = out.shape[0] // order.shape[0]
    for c in range(order.shape[0]):
        at = pl.ds(pl.multiple_of(order[c] * points, points), points)
        out[c * points : (c + 1) * points] = held[at, :].astype(BF16)


def mix_vectors(weights, blocks, each, mixed):
    points = blocks[0].shape[0] // each
    count, _, width = mixed.shape
    for n in range(each):
        at = slice(n * points, (n + 1) * points)
        vectors = jnp.concatenate([block[at] for block in blocks], axis=0)
        value = dot(weights[...], vectors).astype(BF16)
        mixed[:, at, :] = value.reshape(count, points, width)


def through(mixed, kernel_refs):
    total, c = 0.0, 0
    for ref in kernel_refs:
        for k in range(ref.shape[0]):
            total = total + dot(mixed[c], ref[k])
            c += 1
    return total


def row_kernel(each, parts, order, table, vectors_at, *refs):
    kernels, refs = refs[:parts], refs[parts:]
    _, out, vectors, mixed, sems = refs
    points, columns, width = vectors.shape
    count, rows = mixed.shape[:2]
    pieces = sems.shape[0]
    group = columns // pieces
    copies = loads(vectors_at, vectors, sems, pieces, axis=1)
    names = lax.broadcasted_iota(jnp.int32, (points, 1), 0)
    cols = points * each
    wide = dot(table[...], widening(names, cols, each))
    mixer = spread(wide, each, same_column(count * rows * each, cols, each))
    for p in range(pieces):
        copies[p].wait()
        at = slice(p * group, (p + 1) * group)
        value = vectors[:, at, :].astype(F32).reshape(points, group // each, each, width)
        parts = []
        for g in range(group // each):
            flat = value[:, g].reshape(cols, width).astype(BF16)
            parts.append(dot(mixer, flat).reshape(count * rows, each, width))
        joined = jnp.concatenate(parts, axis=1).astype(BF16)
        mixed[:, :, at, :] = joined.reshape(count, rows, group, width)
    total, c = 0.0, 0
    for kernel in kernels:
        for k in range(kernel.shape[0]):
            total = total + dot(mixed[order[c]].reshape(out.shape), kernel[k])
            c += 1
    out[...] = total.astype(BF16)


def row_call(order, mix, vectors, kernels, later):
    count, rows, points = mix.shape
    columns, width = vectors.shape[1:]
    each = 8
    return pl.pallas_call(
        functools.partial(row_kernel, each, len(kernels)),
        in_specs=[SMEM, VMEM, HBM] + [VMEM] * len(kernels) + [ANY],
        out_specs=VMEM,
        out_shape=shaped((rows * columns, width)),
        scratch_shapes=[
            pltpu.VMEM(vectors.shape, BF16),
            pltpu.VMEM((count, rows, columns, width), BF16),
            pltpu.SemaphoreType.DMA((columns // (2 * each),)),
        ],
        compiler_params=params(24),
        cost_estimate=cost(1, 1),
        name="row_call",
    )(order, mix.reshape(count * rows, points), far(vectors), *kernels, later)


def split_rows(rows, width):
    return pltpu.VMEM((width // 128, rows, 128), F32)


def put(ref, value, at=slice(None)):
    for h in range(ref.shape[0]):
        ref[h, at, :] = value[:, h * 128 : (h + 1) * 128]


def get(ref, at=slice(None)):
    return jnp.concatenate([ref[h, at, :] for h in range(ref.shape[0])], axis=1)


def start_kernel(each, index, pick, transform_at, trial_at, live, *refs):
    start_at, mine, my_trial, transform, trial, start, held, rows, sems = refs
    pieces = 4
    load_trial = loads(trial_at, trial, sems, pieces)
    load_transform = loads(transform_at, transform, sems, pieces, first=pieces)
    points, width, _ = transform.shape
    group = points // pieces
    at_mine = pl.ds(pl.multiple_of(index[0] * each, each), each)
    stores = []
    for p in range(pieces):
        load_trial[p].wait()
        load_transform[p].wait()
        for k in range(p * group, (p + 1) * group):
            here = slice(k * each, (k + 1) * each)
            block = trial[k * width : (k + 1) * width, :]
            turned_block = block.astype(F32).T
            vectors = turned_block * live[k : k + 1, :]
            turned = dot(vectors.astype(BF16), transform[k], NT)
            start[k] = turned.astype(BF16)
            if each % 8 == 0:
                rows[0] = turned_block
                rows[1] = turned
                my_trial[here] = rows[0, at_mine, :]
                put(held, rows[1, at_mine, :], pl.ds(k, each, stride=points))
            else:
                my_trial[here] = dot(pick[...], block, NT)
                put(held, dot(pick[...], start[k]), pl.ds(k, each, stride=points))
        store(start, start_at, pl.ds(p * group, group), sems.at[2 * pieces + p], stores)
    mine[...] = get(held).astype(BF16)
    finish(stores)


def start_call(index, pick, transform, trial, live):
    each, columns = pick.shape
    points, width, _ = transform.shape
    mine = (points * each, width)
    return pl.pallas_call(
        functools.partial(start_kernel, each),
        in_specs=[SMEM, VMEM, HBM, HBM, VMEM],
        out_specs=[HBM] + [VMEM] * 2,
        out_shape=[
            far_shaped((points, columns, width)),
            shaped(mine),
            shaped(mine, F32),
        ],
        scratch_shapes=[
            pltpu.VMEM(transform.shape, BF16),
            pltpu.VMEM(trial.shape, BF16),
            pltpu.VMEM((points, columns, width), BF16),
            split_rows(*mine),
            pltpu.VMEM((2, columns, width), F32),
            pltpu.SemaphoreType.DMA((12,)),
        ],
        compiler_params=params(16),
        cost_estimate=cost(4 * points * columns * width * width, 8 * MIB),
        name="start_call",
    )(index, pick, far(transform), far(trial), live)


def fold_kernel(scale, each, place, transform_at, live, energy, my_trial, *refs):
    folded_at, shift, wanted_at, transform, folded, sems = refs
    pieces = 4
    group = transform.shape[0] // pieces
    copies = loads(transform_at, transform, sems, pieces)
    stores = []
    for p in range(pieces):
        copies[p].wait()
        for k in range(p * group, (p + 1) * group):
            here = slice(k * each, (k + 1) * each)
            table = transform[k]
            masked = (table.astype(F32) * (scale * live[k : k + 1, :])).astype(BF16)
            folded[k] = dot(masked, table, NT).astype(BF16)
            vectors = my_trial[here] * (live[k : k + 1, :] * energy[k : k + 1, :])
            shift[here] = dot(vectors.astype(BF16), table, NT)
        store(folded, folded_at, pl.ds(p * group, group), sems.at[pieces + p], stores)
    wanted = transform.at[pl.ds(place[0], wanted_at.shape[0])]
    stores.append(pltpu.make_async_copy(wanted, wanted_at, sems.at[2 * pieces]))
    stores[-1].start()
    finish(stores)


def fold_call(place, rows, transform, live, energy, my_trial, scale, each):
    points, width, _ = transform.shape
    vectors = (points * each, width)
    return pl.pallas_call(
        functools.partial(fold_kernel, scale, each),
        in_specs=[SMEM, HBM] + [VMEM] * 3,
        out_specs=[HBM, VMEM, HBM],
        out_shape=[
            far_shaped(transform.shape),
            shaped(vectors, F32),
            far_shaped((rows, width, width)),
        ],
        scratch_shapes=[
            pltpu.VMEM(transform.shape, BF16),
            pltpu.VMEM(transform.shape, BF16),
            pltpu.SemaphoreType.DMA((9,)),
        ],
        compiler_params=params(16),
        cost_estimate=cost(3 * points * width * width * width, 8 * MIB),
        name="fold_call",
    )(place, far(transform), live, energy, my_trial)


def unpack_kernel(*refs):
    *packed, out = refs
    for c, ref in enumerate(packed):
        out[c] = unpack(ref[...])


def unpack_call(packed, width):
    return pl.pallas_call(
        unpack_kernel,
        in_specs=[VMEM] * len(packed),
        out_specs=VMEM,
        out_shape=shaped((len(packed), width, width)),
        compiler_params=params(16),
        cost_estimate=cost(1, 1),
        name="unpack_call",
    )(*packed)


def first_kernel(each, count, planes, order, names, *refs):
    blocks, refs = refs[:planes], refs[planes:]
    packed, refs = refs[:count], refs[count:]
    early, folded_at, shift, late, total, again, weights, *refs = refs
    mixed, folded, held, wide, sems = refs
    pieces = sems.shape[0]
    copies = loads(folded_at, folded, sems, pieces)
    gathered_weights(order, packed, names, weights.shape[1], wide, weights)
    mix_vectors(weights, blocks, each, mixed)
    for c in range(late.shape[0]):
        late[c] = unpack(packed[early.shape[0] + c][...])
    put(total, through(mixed, [early, late]))
    points = folded.shape[0]
    for k in range(points):
        if k % (points // pieces) == 0:
            copies[k // (points // pieces)].wait()
        rows = pl.ds(k, each, stride=points)
        value = dot(get(total, rows).astype(BF16), folded[k])
        put(held, value + shift[k * each : (k + 1) * each], rows)
    again[...] = get(held).astype(BF16)


def first_call(order, names, blocks, packed, early, folded, shift, each):
    count = len(packed)
    rows, width = blocks[0].shape
    points = rows // each
    fine = points * len(blocks)
    operands = [names, *blocks, *packed, early, far(folded), shift]
    return pl.pallas_call(
        functools.partial(first_kernel, each, count, len(blocks)),
        in_specs=[SMEM] + [VMEM] * (len(operands) - 2) + [HBM, VMEM],
        out_specs=[VMEM] * 4,
        out_shape=[
            shaped((count - early.shape[0], width, width)),
            shaped((width // 128, rows, 128), F32),
            shaped((rows, width)),
            shaped((count * points, fine)),
        ],
        scratch_shapes=[
            pltpu.VMEM((count, rows, width), BF16),
            pltpu.VMEM(folded.shape, BF16),
            split_rows(rows, width),
            pltpu.VMEM((count * points, fine), F32),
            pltpu.SemaphoreType.DMA((8,)),
        ],
        compiler_params=params(20),
        cost_estimate=cost(1, 1),
        name="first_call",
    )(order, *operands)


def energy_kernel(scale, each, transform_at, total, live, energy, trial, out, transform, sems):
    pieces = sems.shape[0]
    copies = loads(transform_at, transform, sems, pieces)
    points = transform.shape[0]
    for k in range(points):
        if k % (points // pieces) == 0:
            copies[k // (points // pieces)].wait()
        here = slice(k * each, (k + 1) * each)
        turned = dot(get(total, pl.ds(k, each, stride=points)).astype(BF16), transform[k])
        row = energy[k : k + 1, :]
        out[here] = (turned * (scale * live[k : k + 1, :]) + row * trial[here]) * row


def energy_call(transform, total, live, energy, my_trial, scale, each):
    return pl.pallas_call(
        functools.partial(energy_kernel, scale, each),
        in_specs=[HBM] + [VMEM] * 4,
        out_specs=VMEM,
        out_shape=shaped(my_trial.shape, F32),
        scratch_shapes=[pltpu.VMEM(transform.shape, BF16), pltpu.SemaphoreType.DMA((4,))],
        compiler_params=params(16),
        cost_estimate=cost(1, 1),
        name="energy_call",
    )(far(transform), total, live, energy, my_trial)


def second_kernel(scale, each, planes, weights, *refs):
    blocks, refs = refs[:planes], refs[planes:]
    early, late, transform_at, live, shift, out, mixed, transform, total, held, sems = refs
    pieces = sems.shape[0]
    copies = loads(transform_at, transform, sems, pieces)
    mix_vectors(weights, blocks, each, mixed)
    put(total, through(mixed, [early, late]))
    points = transform.shape[0]
    for k in range(points):
        if k % (points // pieces) == 0:
            copies[k // (points // pieces)].wait()
        here = slice(k * each, (k + 1) * each)
        turned = dot(get(total, pl.ds(k, each, stride=points)).astype(BF16), transform[k])
        held[here] = turned * (scale * live[k : k + 1, :]) + shift[here]
    out[...] = held[...].astype(BF16)


def second_call(weights, blocks, kernels, transform, live, shift, scale, each):
    rows, width = shift.shape
    count = sum(kernel.shape[0] for kernel in kernels)
    operands = [weights, *blocks, *kernels, far(transform), live, shift]
    return pl.pallas_call(
        functools.partial(second_kernel, scale, each, len(blocks)),
        in_specs=[VMEM] * (len(operands) - 3) + [HBM, VMEM, VMEM],
        out_specs=VMEM,
        out_shape=shaped((rows, width)),
        scratch_shapes=[
            pltpu.VMEM((count, rows, width), BF16),
            pltpu.VMEM(transform.shape, BF16),
            split_rows(rows, width),
            pltpu.VMEM((rows, width), F32),
            pltpu.SemaphoreType.DMA((8,)),
        ],
        compiler_params=params(20),
        cost_estimate=cost(1, 1),
        name="second_call",
    )(*operands)


def last_kernel(each, order, trial_at, *refs):
    *blocks, out_at, held, trial, out, in_sems, out_sems, sems = refs
    pieces = out_sems.shape[0]
    copies = [
        pltpu.make_async_copy(block, held.at[order[r]], sems.at[r])
        for r, block in enumerate(blocks)
    ]
    for copy in copies:
        copy.start()
    load_trial = loads(trial_at, trial, in_sems, pieces)
    finish(copies)
    width, columns = held.shape[2], trial.shape[1]
    points = trial.shape[0] // width // pieces
    stores = []
    for p in range(pieces):
        load_trial[p].wait()
        part = held[:, p * points * each : (p + 1) * points * each, :].astype(F32)
        part = part.reshape(len(blocks), points, each, width)
        for k in range(points):
            rows = part[:, k].reshape(columns, width)
            first = (p * points + k) * width
            at = slice(first, first + width)
            out[at] = 2.0 * rows.T - trial[at].astype(F32)
        at = pl.ds(p * points * width, points * width)
        store(out, out_at, at, out_sems.at[p], stores)
    finish(stores)


def last_call(blocks, order, trial, each):
    total, columns = trial.shape
    rows, width = blocks[0].shape
    if each % 8 != 0:
        place = jnp.zeros_like(order).at[order].set(jnp.arange(order.shape[0], dtype=jnp.int32))
        held = jnp.stack(blocks)[place].reshape(len(blocks), -1, each, width)
        summed = jnp.transpose(held, (1, 3, 0, 2)).reshape(total, columns)
        return 2.0 * summed.astype(F32) - trial.astype(F32)
    pieces = 8
    return pl.pallas_call(
        functools.partial(last_kernel, each),
        in_specs=[SMEM, HBM] + [HBM] * len(blocks),
        out_specs=HBM,
        out_shape=shaped((total, columns), F32),
        scratch_shapes=[
            pltpu.VMEM((len(blocks), rows, width), BF16),
            pltpu.VMEM((total, columns), BF16),
            pltpu.VMEM((total, columns), F32),
            pltpu.SemaphoreType.DMA((pieces,)),
            pltpu.SemaphoreType.DMA((pieces,)),
            pltpu.SemaphoreType.DMA((len(blocks),)),
        ],
        compiler_params=params(24),
        cost_estimate=cost(2 * total * columns * width, 8 * MIB),
        name="last_call",
    )(order, far(trial), *[far(block) for block in blocks])


def shards(screened, density, transform, energy, trial, coarse_index, interp_weight, bands):
    pair_count = lax.axis_size("pair")
    plane_count = lax.axis_size("pw")
    row_index = lax.axis_index("pair")
    col_index = lax.axis_index("pw")
    transitions = density.shape[2]
    row_points, col_points, neighbours = coarse_index.shape
    fine_points = bands.shape[0]
    columns = trial.shape[1]
    each = columns // pair_count
    norm_scale = 1.0 / math.sqrt(fine_points * transitions)
    order = pair_order().astype(jnp.int32)

    density_blocks = plane_blocks(density[0])

    names = jnp.arange(pair_count, dtype=jnp.int32)
    hit = jnp.swapaxes(coarse_index, 1, 2)[:, None, :, :] == names[None, :, None, None]
    weight = jnp.swapaxes(interp_weight, 1, 2).astype(F32)[:, None, :, :]
    dense = jnp.sum(jnp.where(hit, weight, 0.0), axis=2).astype(BF16)

    positions = jnp.arange(transitions) % NCOND
    live = (positions[None, :] < bands[:, None]).astype(F32)
    my_live = lax.dynamic_slice_in_dim(live, col_index * col_points, col_points, 0)
    energies = energy.reshape(col_points, transitions)
    pick = (
        jnp.arange(columns)[None, :] == row_index * each + jnp.arange(each)[:, None]
    ).astype(BF16)

    start, my_start, my_trial = start_call(
        row_index[None].astype(jnp.int32), pick, transform, trial, my_live
    )

    planes = jnp.stack([(col_index + d) % plane_count for d in range(plane_count)])
    planes = planes.astype(jnp.int32)
    first_point = row_index * row_points
    place = (first_point % col_points).astype(jnp.int32)
    left, own = left_product(planes[:1], screened, density[0], my_start)
    folded, shift, wanted = fold_call(
        place[None], row_points, transform, my_live, energies, my_trial, norm_scale, each
    )
    packed = coarse_block(planes[1:], left, own, density_blocks[1:], (shift, my_start))
    packed = plane_sum(packed).astype(BF16)

    table = dense.reshape(row_points, -1)
    chunks = table.shape[1] // packed.shape[1]
    table = table.reshape(row_points * chunks, packed.shape[1])
    start_blocks = plane_blocks(after(my_start, packed))
    blocks, _ = pair_blocks(jnp.concatenate([packed, table], axis=0), first=start_blocks[1:])
    names = jnp.arange(fine_points, dtype=jnp.int32).reshape(pair_count, row_points)[order]
    names = (jnp.repeat(names, chunks, axis=1) - col_index * col_points) % fine_points
    names = names.reshape(-1, 1)

    early = unpack_call(blocks[: len(pair_moves()[0])], transitions)
    late, total, again, weights = first_call(
        order, names, start_blocks, blocks, early, folded, shift, each
    )
    kernels = [early, late]
    again_blocks = plane_blocks(again)
    energy_part = energy_call(transform, total, my_live, energies, my_trial, norm_scale, each)

    second = second_call(
        weights, again_blocks, kernels, transform, my_live, energy_part, norm_scale, each
    )
    by_point_first = jnp.swapaxes(dense, 0, 1)
    second_blocks, row_back = pair_blocks(
        second, lambda block: row_call(order, by_point_first, start, kernels, block)
    )

    wanted_blocks = plane_blocks(after(wanted, second))
    root = first_point // col_points
    row_transform = wanted
    for step in range(1, plane_count):
        from_root = (col_index + step) % plane_count == root
        row_transform = jnp.where(from_root, wanted_blocks[step], row_transform)
    row_back = row_back.reshape(row_points, columns, transitions)
    row_part = jnp.einsum("ksv,kns->kvn", row_transform, row_back, preferred_element_type=F32)
    row_live = lax.dynamic_slice_in_dim(live, first_point, row_points, 0)
    row_energy = lax.dynamic_slice_in_dim(energies, first_point % col_points, row_points, 0)
    trial_blocks = trial.reshape(col_points, transitions, columns)
    row_trial = lax.dynamic_slice_in_dim(trial_blocks, first_point % col_points, row_points, 0)
    diagonal = jnp.where(root == col_index, row_energy[:, :, None] * row_trial.astype(F32), 0.0)
    row_part = row_part * norm_scale * row_live[:, :, None] + diagonal
    first_step = plane_sum(row_part.astype(BF16)).astype(BF16)
    first_step = first_step.reshape(row_points * transitions, columns)

    second_step = last_call(second_blocks, order, trial, each)
    return (first_step, second_step)


def solution(mesh):
    in_specs = (
        P("pair", "pw", None),
        P("pair", "pw", None),
        P("pw", None, None),
        P("pw"),
        P("pw", None),
        P("pair", "pw", None),
        P("pair", "pw", None),
        P(),
    )
    out_specs = (P("pair", None), P("pw", None))
    return jax.shard_map(shards, mesh=mesh, in_specs=in_specs, out_specs=out_specs, check_vma=False)
```

```python
import functools
import math

import jax
import jax.numpy as jnp
from jax import lax
from jax.experimental import pallas as pl
from jax.experimental.pallas import tpu as pltpu
from jax.sharding import PartitionSpec as P

NCOND = 16
F32 = jnp.float32
BF16 = jnp.bfloat16
MIB = 1 << 20
NN = (((1,), (0,)), ((), ()))
NT = (((1,), (1,)), ((), ()))
TN = (((0,), (0,)), ((), ()))


def dot(a, b, dims=NN):
    return lax.dot_general(a, b, dims, preferred_element_type=F32)


def cost(flops, read):
    return pl.CostEstimate(flops=1, bytes_accessed=1, transcendentals=0)


def params(mib):
    return pltpu.CompilerParams(vmem_limit_bytes=mib * MIB)


def whole(shape):
    return pl.BlockSpec(shape, lambda *_: (0,) * len(shape))


ANY = pl.BlockSpec(memory_space=pl.ANY)
HBM = pl.BlockSpec(memory_space=pltpu.HBM)
VMEM = pl.BlockSpec(memory_space=pltpu.VMEM)
SMEM = pl.BlockSpec(memory_space=pltpu.SMEM)


def far(value):
    return pltpu.with_memory_space_constraint(value, pltpu.HBM)


def shaped(shape, dtype=BF16):
    return jax.ShapeDtypeStruct(shape, dtype)


def far_shaped(shape):
    return pltpu.HBM(shape, BF16)


def loads(source, target, sems, pieces, axis=0, first=0):
    size = target.shape[axis] // pieces
    copies = []
    for p in range(pieces):
        at = (slice(None),) * axis + (pl.ds(p * size, size),)
        copies.append(pltpu.make_async_copy(source.at[at], target.at[at], sems.at[first + p]))
        copies[-1].start()
    return copies


def store(source, target, at, sem, copies):
    copies.append(pltpu.make_async_copy(source.at[at], target.at[at], sem))
    copies[-1].start()


def finish(copies):
    for copy in copies:
        copy.wait()


def from_ahead(value, axis, step):
    count = lax.axis_size(axis)
    return lax.ppermute(value, axis, [((s + step) % count, s) for s in range(count)])


def flipped(value, axis, bit):
    count = lax.axis_size(axis)
    return lax.ppermute(value, axis, [(s, s ^ bit) for s in range(count)])


def plane_blocks(value):
    return [value] + [from_ahead(value, "pw", d) for d in range(1, lax.axis_size("pw"))]


def pair_moves():
    groups = lax.axis_size("pair") // 4
    far = sorted(range(groups), key=lambda d: min(d, groups - d))
    early = [(d, 0, 0) for d in far] + [(0, 1, 0)] + [(d, 0, 1) for d in far] + [(0, 1, 1)]
    early += [(d, 1, 0) for d in far[1:-1]]
    late = [(d, 1, 1) for d in far[1:-1]] + [(far[-1], 1, 0), (far[-1], 1, 1)]
    return early, late


def after(value, *others):
    return lax.optimization_barrier((value, *others))[0]


def pair_blocks(value, meanwhile=None, first=()):
    early, late = pair_moves()
    far_moves = [move for move in early if move[0] and not move[1] and not move[2]]
    held = {(0, 0, 0): value, (0, 1, 0): flipped(value, "pair", 2)}
    for move in far_moves:
        ready = value
        if meanwhile is None and move == far_moves[-1]:
            ready = after(value, *[held[other] for other in far_moves[:-1]])
        held[move] = from_ahead(ready, "pair", 4 * move[0])
    if first:
        held[far_moves[-1]] = after(held[far_moves[-1]], *first)
    done = None
    if meanwhile is not None:
        done = meanwhile(held[0, 1, 0])
        for move in far_moves:
            held[move] = after(held[move], done)
    for move in early + late:
        far, side, core = move
        if core and move not in held:
            held[move] = flipped(held[far, side, 0], "pair", 1)
        elif side and far and not core:
            held[move] = flipped(held[far, 0, 0], "pair", 2)
    return [held[move] for move in early + late], done


def pair_order():
    early, late = pair_moves()
    me = lax.axis_index("pair")
    count = lax.axis_size("pair")
    return jnp.stack([((me + 4 * far) % count) ^ (2 * side + core) for far, side, core in early + late])


def plane_sum(value):
    blocks = plane_blocks(value)
    if len(blocks) == 2:
        return blocks[0].astype(F32) + blocks[1].astype(F32)
    stacked = jnp.roll(jnp.stack(blocks), lax.axis_index("pw"), axis=0)
    return jnp.sum(stacked.astype(F32), axis=0)


def iotas(rows, cols):
    return (
        lax.broadcasted_iota(jnp.int32, (rows, cols), 0),
        lax.broadcasted_iota(jnp.int32, (rows, cols), 1),
    )


def pack(symmetric, out):
    half = symmetric.shape[0] // 2
    row, col = iotas(half, half)
    upper, lower = symmetric[:half, :half], symmetric[half:, half:]
    diagonal = jnp.sum(jnp.where(row == col, upper, 0.0), axis=0, keepdims=True)
    out[:half] = symmetric[:half, half:].astype(BF16)
    out[half : 2 * half] = jnp.where(row > col, upper, lower).astype(BF16)
    out[2 * half :] = jnp.broadcast_to(diagonal, (16, half)).astype(BF16)


def unpack(packed):
    half = packed.shape[1]
    row, col = iotas(half, half)
    corner = packed[:half]
    both = packed[half : 2 * half].astype(F32)
    diagonal = packed[2 * half : 2 * half + 1].astype(F32)
    other = both.T
    upper = jnp.where(row > col, both, jnp.where(row == col, diagonal, other))
    lower = jnp.where(row <= col, both, other)
    top = jnp.concatenate([upper.astype(BF16), corner], axis=1)
    bottom = jnp.concatenate([corner.T, lower.astype(BF16)], axis=1)
    return jnp.concatenate([top, bottom], axis=0)


def left_kernel(planes, screened_at, density, _, out, total, screened, turned, left, sems):
    pieces = sems.shape[0]
    copies = loads(screened_at.at[0], screened, sems, pieces, axis=1)
    rows = density.shape[0]
    turned[...] = density[...].T
    size = left.shape[1] // pieces
    for p in range(pieces):
        copies[p].wait()
        at = slice(p * size, (p + 1) * size)
        left[:, at] = dot(turned[...], screened[:, at]).astype(BF16)
    at = pl.multiple_of(planes[0] * rows, rows)
    total[...] = dot(left[:, pl.ds(at, rows)], density[...])
    for step in range(out.shape[0]):
        at = pl.multiple_of(planes[step + 1] * rows, rows)
        out[step] = left[:, pl.ds(at, rows)]


def left_product(planes, screened, density, later):
    rows, width = density.shape
    depth = screened.shape[2]
    return pl.pallas_call(
        left_kernel,
        in_specs=[SMEM, HBM, VMEM, ANY],
        out_specs=[VMEM, VMEM],
        out_shape=[shaped((depth // rows - 1, width, rows)), shaped((width, width), F32)],
        scratch_shapes=[
            pltpu.VMEM((rows, depth), BF16),
            pltpu.VMEM((width, rows), BF16),
            pltpu.VMEM((width, depth), BF16),
            pltpu.SemaphoreType.DMA((8,)),
        ],
        compiler_params=params(24),
        cost_estimate=cost(1, 1),
        name="left_product",
    )(planes, far(screened), density, later)


def coarse_kernel(left, total, *refs):
    *blocks, _, _, out = refs
    raw = total[...]
    for step, block in enumerate(blocks):
        raw = raw + dot(left[step], block[...])
    pack(0.5 * (raw + raw.T), out)


def coarse_block(left, total, density_blocks, later):
    width = left.shape[1]
    return pl.pallas_call(
        coarse_kernel,
        in_specs=[VMEM] * (2 + len(density_blocks)) + [ANY] * 2,
        out_specs=VMEM,
        out_shape=shaped((width + 16, width // 2)),
        compiler_params=params(16),
        cost_estimate=cost(1, 1),
        name="coarse_block",
    )(left, total, *density_blocks, *later)


def spread(table, each, same):
    rows, cols = table.shape
    tall = jnp.broadcast_to(table[:, None, :], (rows, each, cols)).reshape(rows * each, cols)
    return (tall * same).astype(BF16)


def same_column(rows, cols, each):
    row, col = iotas(rows, cols)
    return jnp.where(((row ^ col) & (each - 1)) == 0, 1.0, 0.0)


def widening(names, cols, each):
    col = lax.broadcasted_iota(jnp.int32, (names.shape[0], cols), 1)
    return jnp.where((col >= names * each) & (col < (names + 1) * each), 1.0, 0.0).astype(BF16)


def gathered_weights(order, tables, names, fine, held, out):
    rows = names.shape[0] // len(tables)
    table = jnp.concatenate([ref[ref.shape[0] - rows :, :] for ref in tables], axis=0)
    chunks = out.shape[0] // table.shape[1]
    row = lax.broadcasted_iota(jnp.int32, names.shape, 0)
    col = lax.broadcasted_iota(jnp.int32, (names.shape[0], fine), 1)
    for p in range(chunks):
        here = jnp.where(row % chunks == p, names[...], -1)
        place = jnp.where(col == here, 1.0, 0.0).astype(BF16)
        at = slice(p * table.shape[1], (p + 1) * table.shape[1])
        held[at] = dot(table, place, TN)
    points = out.shape[0] // order.shape[0]
    for c in range(order.shape[0]):
        at = pl.ds(pl.multiple_of(order[c] * points, points), points)
        out[c * points : (c + 1) * points] = held[at, :].astype(BF16)


def mix_vectors(weights, blocks, each, mixed):
    points = blocks[0].shape[0] // each
    count, _, width = mixed.shape
    for n in range(each):
        at = slice(n * points, (n + 1) * points)
        vectors = jnp.concatenate([block[at] for block in blocks], axis=0)
        value = dot(weights[...], vectors).astype(BF16)
        mixed[:, at, :] = value.reshape(count, points, width)


def through(mixed, kernel_refs):
    total, c = 0.0, 0
    for ref in kernel_refs:
        for k in range(ref.shape[0]):
            total = total + dot(mixed[c], ref[k])
            c += 1
    return total


def row_kernel(each, parts, order, table, vectors_at, *refs):
    kernels, refs = refs[:parts], refs[parts:]
    _, out, vectors, mixed, held, mixer, sems = refs
    points, columns, width = vectors.shape
    count, rows = mixed.shape[:2]
    pieces = columns // (2 * each)
    group = columns // pieces
    copies = loads(vectors_at, vectors, sems, sems.shape[0])
    names = lax.broadcasted_iota(jnp.int32, (points, 1), 0)
    cols = points * each
    wide = dot(table[...], widening(names, cols, each))
    held[...] = spread(wide, each, same_column(count * rows * each, cols, each)).astype(F32)
    size = rows * each
    for c in range(count):
        at = pl.ds(pl.multiple_of(order[c] * size, size), size)
        mixer[c * size : (c + 1) * size] = held[at, :].astype(BF16)
    finish(copies)
    for p in range(pieces):
        at = slice(p * group, (p + 1) * group)
        value = vectors[:, at, :].astype(F32).reshape(points, group // each, each, width)
        parts = []
        for g in range(group // each):
            flat = value[:, g].reshape(cols, width).astype(BF16)
            parts.append(dot(mixer[...], flat).reshape(count * rows, each, width))
        joined = jnp.concatenate(parts, axis=1).astype(BF16)
        mixed[:, :, at, :] = joined.reshape(count, rows, group, width)
    total, c = 0.0, 0
    for kernel in kernels:
        for k in range(kernel.shape[0]):
            total = total + dot(mixed[c].reshape(out.shape), kernel[k])
            c += 1
    out[...] = total.astype(BF16)


def row_call(order, mix, vectors, kernels, later):
    count, rows, points = mix.shape
    columns, width = vectors.shape[1:]
    each = 8
    return pl.pallas_call(
        functools.partial(row_kernel, each, len(kernels)),
        in_specs=[SMEM, VMEM, HBM] + [VMEM] * len(kernels) + [ANY],
        out_specs=VMEM,
        out_shape=shaped((rows * columns, width)),
        scratch_shapes=[
            pltpu.VMEM(vectors.shape, BF16),
            pltpu.VMEM((count, rows, columns, width), BF16),
            pltpu.VMEM((count * rows * each, points * each), F32),
            pltpu.VMEM((count * rows * each, points * each), BF16),
            pltpu.SemaphoreType.DMA((4,)),
        ],
        compiler_params=params(24),
        cost_estimate=cost(1, 1),
        name="row_call",
    )(order, mix.reshape(count * rows, points), far(vectors), *kernels, later)


def split_rows(rows, width):
    return pltpu.VMEM((width // 128, rows, 128), F32)


def put(ref, value, at=slice(None)):
    for h in range(ref.shape[0]):
        ref[h, at, :] = value[:, h * 128 : (h + 1) * 128]


def get(ref, at=slice(None)):
    return jnp.concatenate([ref[h, at, :] for h in range(ref.shape[0])], axis=1)


def start_kernel(each, index, pick, transform_at, trial_at, live, *refs):
    start_at, mine, my_trial, transform, trial, start, held, rows, sems = refs
    pieces = 4
    load_trial = loads(trial_at, trial, sems, pieces)
    load_transform = loads(transform_at, transform, sems, pieces, first=pieces)
    points, width, _ = transform.shape
    group = points // pieces
    at_mine = pl.ds(pl.multiple_of(index[0] * each, each), each)
    stores = []
    for p in range(pieces):
        load_trial[p].wait()
        load_transform[p].wait()
        for k in range(p * group, (p + 1) * group):
            here = slice(k * each, (k + 1) * each)
            block = trial[k * width : (k + 1) * width, :]
            turned_block = block.astype(F32).T
            vectors = turned_block * live[k : k + 1, :]
            turned = dot(vectors.astype(BF16), transform[k], NT)
            start[k] = turned.astype(BF16)
            if each % 8 == 0:
                rows[0] = turned_block
                rows[1] = turned
                my_trial[here] = rows[0, at_mine, :]
                put(held, rows[1, at_mine, :], pl.ds(k, each, stride=points))
            else:
                my_trial[here] = dot(pick[...], block, NT)
                put(held, dot(pick[...], start[k]), pl.ds(k, each, stride=points))
        store(start, start_at, pl.ds(p * group, group), sems.at[2 * pieces + p], stores)
    mine[...] = get(held).astype(BF16)
    finish(stores)


def start_call(index, pick, transform, trial, live):
    each, columns = pick.shape
    points, width, _ = transform.shape
    mine = (points * each, width)
    return pl.pallas_call(
        functools.partial(start_kernel, each),
        in_specs=[SMEM, VMEM, HBM, HBM, VMEM],
        out_specs=[HBM] + [VMEM] * 2,
        out_shape=[
            far_shaped((points, columns, width)),
            shaped(mine),
            shaped(mine, F32),
        ],
        scratch_shapes=[
            pltpu.VMEM(transform.shape, BF16),
            pltpu.VMEM(trial.shape, BF16),
            pltpu.VMEM((points, columns, width), BF16),
            split_rows(*mine),
            pltpu.VMEM((2, columns, width), F32),
            pltpu.SemaphoreType.DMA((12,)),
        ],
        compiler_params=params(16),
        cost_estimate=cost(4 * points * columns * width * width, 8 * MIB),
        name="start_call",
    )(index, pick, far(transform), far(trial), live)


def fold_kernel(scale, each, place, transform_at, live, energy, my_trial, *refs):
    folded_at, shift, wanted_at, transform, folded, sems = refs
    pieces = 4
    group = transform.shape[0] // pieces
    copies = loads(transform_at, transform, sems, pieces)
    stores = []
    for p in range(pieces):
        copies[p].wait()
        for k in range(p * group, (p + 1) * group):
            here = slice(k * each, (k + 1) * each)
            table = transform[k]
            masked = (table.astype(F32) * (scale * live[k : k + 1, :])).astype(BF16)
            folded[k] = dot(masked, table, NT).astype(BF16)
            vectors = my_trial[here] * (live[k : k + 1, :] * energy[k : k + 1, :])
            shift[here] = dot(vectors.astype(BF16), table, NT)
        store(folded, folded_at, pl.ds(p * group, group), sems.at[pieces + p], stores)
    wanted = transform.at[pl.ds(place[0], wanted_at.shape[0])]
    stores.append(pltpu.make_async_copy(wanted, wanted_at, sems.at[2 * pieces]))
    stores[-1].start()
    finish(stores)


def fold_call(place, rows, transform, live, energy, my_trial, scale, each):
    points, width, _ = transform.shape
    vectors = (points * each, width)
    return pl.pallas_call(
        functools.partial(fold_kernel, scale, each),
        in_specs=[SMEM, HBM] + [VMEM] * 3,
        out_specs=[HBM, VMEM, HBM],
        out_shape=[
            far_shaped(transform.shape),
            shaped(vectors, F32),
            far_shaped((rows, width, width)),
        ],
        scratch_shapes=[
            pltpu.VMEM(transform.shape, BF16),
            pltpu.VMEM(transform.shape, BF16),
            pltpu.SemaphoreType.DMA((9,)),
        ],
        compiler_params=params(16),
        cost_estimate=cost(3 * points * width * width * width, 8 * MIB),
        name="fold_call",
    )(place, far(transform), live, energy, my_trial)


def unpack_kernel(*refs):
    *packed, out = refs
    for c, ref in enumerate(packed):
        out[c] = unpack(ref[...])


def unpack_call(packed, width):
    return pl.pallas_call(
        unpack_kernel,
        in_specs=[VMEM] * len(packed),
        out_specs=VMEM,
        out_shape=shaped((len(packed), width, width)),
        compiler_params=params(16),
        cost_estimate=cost(1, 1),
        name="unpack_call",
    )(*packed)


def first_kernel(each, count, planes, order, names, *refs):
    blocks, refs = refs[:planes], refs[planes:]
    packed, refs = refs[:count], refs[count:]
    early, folded_at, shift, late, total, again, weights, *refs = refs
    mixed, folded, held, wide, sems = refs
    pieces = sems.shape[0]
    copies = loads(folded_at, folded, sems, pieces)
    gathered_weights(order, packed, names, weights.shape[1], wide, weights)
    mix_vectors(weights, blocks, each, mixed)
    for c in range(late.shape[0]):
        late[c] = unpack(packed[early.shape[0] + c][...])
    put(total, through(mixed, [early, late]))
    points = folded.shape[0]
    for k in range(points):
        if k % (points // pieces) == 0:
            copies[k // (points // pieces)].wait()
        rows = pl.ds(k, each, stride=points)
        value = dot(get(total, rows).astype(BF16), folded[k])
        put(held, value + shift[k * each : (k + 1) * each], rows)
    again[...] = get(held).astype(BF16)


def first_call(order, names, blocks, packed, early, folded, shift, each):
    count = len(packed)
    rows, width = blocks[0].shape
    points = rows // each
    fine = points * len(blocks)
    operands = [names, *blocks, *packed, early, far(folded), shift]
    return pl.pallas_call(
        functools.partial(first_kernel, each, count, len(blocks)),
        in_specs=[SMEM] + [VMEM] * (len(operands) - 2) + [HBM, VMEM],
        out_specs=[VMEM] * 4,
        out_shape=[
            shaped((count - early.shape[0], width, width)),
            shaped((width // 128, rows, 128), F32),
            shaped((rows, width)),
            shaped((count * points, fine)),
        ],
        scratch_shapes=[
            pltpu.VMEM((count, rows, width), BF16),
            pltpu.VMEM(folded.shape, BF16),
            split_rows(rows, width),
            pltpu.VMEM((count * points, fine), F32),
            pltpu.SemaphoreType.DMA((8,)),
        ],
        compiler_params=params(20),
        cost_estimate=cost(1, 1),
        name="first_call",
    )(order, *operands)


def energy_kernel(scale, each, transform_at, total, live, energy, trial, out, transform, sems):
    pieces = sems.shape[0]
    copies = loads(transform_at, transform, sems, pieces)
    points = transform.shape[0]
    for k in range(points):
        if k % (points // pieces) == 0:
            copies[k // (points // pieces)].wait()
        here = slice(k * each, (k + 1) * each)
        turned = dot(get(total, pl.ds(k, each, stride=points)).astype(BF16), transform[k])
        row = energy[k : k + 1, :]
        out[here] = (turned * (scale * live[k : k + 1, :]) + row * trial[here]) * row


def energy_call(transform, total, live, energy, my_trial, scale, each):
    return pl.pallas_call(
        functools.partial(energy_kernel, scale, each),
        in_specs=[HBM] + [VMEM] * 4,
        out_specs=VMEM,
        out_shape=shaped(my_trial.shape, F32),
        scratch_shapes=[pltpu.VMEM(transform.shape, BF16), pltpu.SemaphoreType.DMA((4,))],
        compiler_params=params(16),
        cost_estimate=cost(1, 1),
        name="energy_call",
    )(far(transform), total, live, energy, my_trial)


def second_kernel(scale, each, planes, weights, *refs):
    blocks, refs = refs[:planes], refs[planes:]
    early, late, transform_at, live, shift, out, mixed, transform, total, held, sems = refs
    pieces = sems.shape[0]
    copies = loads(transform_at, transform, sems, pieces)
    mix_vectors(weights, blocks, each, mixed)
    put(total, through(mixed, [early, late]))
    points = transform.shape[0]
    for k in range(points):
        if k % (points // pieces) == 0:
            copies[k // (points // pieces)].wait()
        here = slice(k * each, (k + 1) * each)
        turned = dot(get(total, pl.ds(k, each, stride=points)).astype(BF16), transform[k])
        held[here] = turned * (scale * live[k : k + 1, :]) + shift[here]
    out[...] = held[...].astype(BF16)


def second_call(weights, blocks, kernels, transform, live, shift, scale, each):
    rows, width = shift.shape
    count = sum(kernel.shape[0] for kernel in kernels)
    operands = [weights, *blocks, *kernels, far(transform), live, shift]
    return pl.pallas_call(
        functools.partial(second_kernel, scale, each, len(blocks)),
        in_specs=[VMEM] * (len(operands) - 3) + [HBM, VMEM, VMEM],
        out_specs=VMEM,
        out_shape=shaped((rows, width)),
        scratch_shapes=[
            pltpu.VMEM((count, rows, width), BF16),
            pltpu.VMEM(transform.shape, BF16),
            split_rows(rows, width),
            pltpu.VMEM((rows, width), F32),
            pltpu.SemaphoreType.DMA((8,)),
        ],
        compiler_params=params(20),
        cost_estimate=cost(1, 1),
        name="second_call",
    )(*operands)


def last_kernel(each, order, trial_at, *refs):
    *blocks, out_at, held, trial, out, in_sems, out_sems, sems = refs
    pieces = out_sems.shape[0]
    copies = [
        pltpu.make_async_copy(block, held.at[order[r]], sems.at[r])
        for r, block in enumerate(blocks)
    ]
    for copy in copies:
        copy.start()
    load_trial = loads(trial_at, trial, in_sems, pieces)
    finish(copies)
    width, columns = held.shape[2], trial.shape[1]
    points = trial.shape[0] // width // pieces
    stores = []
    for p in range(pieces):
        load_trial[p].wait()
        part = held[:, p * points * each : (p + 1) * points * each, :].astype(F32)
        part = part.reshape(len(blocks), points, each, width)
        for k in range(points):
            rows = part[:, k].reshape(columns, width)
            first = (p * points + k) * width
            at = slice(first, first + width)
            out[at] = 2.0 * rows.T - trial[at].astype(F32)
        at = pl.ds(p * points * width, points * width)
        store(out, out_at, at, out_sems.at[p], stores)
    finish(stores)


def last_call(blocks, at_hand, order, trial, each):
    total, columns = trial.shape
    rows, width = blocks[0].shape
    if each % 8 != 0:
        place = jnp.zeros_like(order).at[order].set(jnp.arange(order.shape[0], dtype=jnp.int32))
        held = jnp.stack(blocks)[place].reshape(len(blocks), -1, each, width)
        summed = jnp.transpose(held, (1, 3, 0, 2)).reshape(total, columns)
        return 2.0 * summed.astype(F32) - trial.astype(F32)
    pieces = 8
    return pl.pallas_call(
        functools.partial(last_kernel, each),
        in_specs=[SMEM, HBM] + [ANY] * len(blocks),
        out_specs=HBM,
        out_shape=shaped((total, columns), F32),
        scratch_shapes=[
            pltpu.VMEM((len(blocks), rows, width), BF16),
            pltpu.VMEM((total, columns), BF16),
            pltpu.VMEM((total, columns), F32),
            pltpu.SemaphoreType.DMA((pieces,)),
            pltpu.SemaphoreType.DMA((pieces,)),
            pltpu.SemaphoreType.DMA((len(blocks),)),
        ],
        compiler_params=params(24),
        cost_estimate=cost(2 * total * columns * width, 8 * MIB),
        name="last_call",
    )(order, far(trial), *[b if i in at_hand else far(b) for i, b in enumerate(blocks)])


def shards(screened, density, transform, energy, trial, coarse_index, interp_weight, bands):
    pair_count = lax.axis_size("pair")
    plane_count = lax.axis_size("pw")
    row_index = lax.axis_index("pair")
    col_index = lax.axis_index("pw")
    transitions = density.shape[2]
    row_points, col_points, neighbours = coarse_index.shape
    fine_points = bands.shape[0]
    columns = trial.shape[1]
    each = columns // pair_count
    norm_scale = 1.0 / math.sqrt(fine_points * transitions)
    order = pair_order().astype(jnp.int32)

    density_blocks = plane_blocks(density[0])

    names = jnp.arange(pair_count, dtype=jnp.int32)
    hit = jnp.swapaxes(coarse_index, 1, 2)[:, None, :, :] == names[None, :, None, None]
    weight = jnp.swapaxes(interp_weight, 1, 2).astype(F32)[:, None, :, :]
    dense = jnp.sum(jnp.where(hit, weight, 0.0), axis=2).astype(BF16)

    positions = jnp.arange(transitions) % NCOND
    live = (positions[None, :] < bands[:, None]).astype(F32)
    my_live = lax.dynamic_slice_in_dim(live, col_index * col_points, col_points, 0)
    energies = energy.reshape(col_points, transitions)
    pick = (
        jnp.arange(columns)[None, :] == row_index * each + jnp.arange(each)[:, None]
    ).astype(BF16)

    start, my_start, my_trial = start_call(
        row_index[None].astype(jnp.int32), pick, transform, trial, my_live
    )

    planes = jnp.stack([(col_index + d) % plane_count for d in range(plane_count)])
    planes = planes.astype(jnp.int32)
    first_point = row_index * row_points
    place = (first_point % col_points).astype(jnp.int32)
    left, own = left_product(planes, screened, density[0], my_start)
    folded, shift, wanted = fold_call(
        place[None], row_points, transform, my_live, energies, my_trial, norm_scale, each
    )
    packed = coarse_block(left, own, density_blocks[1:], (shift, my_start))
    packed = plane_sum(packed).astype(BF16)

    table = dense.reshape(row_points, -1)
    chunks = table.shape[1] // packed.shape[1]
    table = table.reshape(row_points * chunks, packed.shape[1])
    start_blocks = plane_blocks(after(my_start, packed))
    blocks, _ = pair_blocks(jnp.concatenate([packed, table], axis=0), first=start_blocks[1:])
    names = order[:, None] * row_points + jnp.arange(row_points * chunks)[None, :] // chunks
    names = (names - col_index * col_points) % fine_points
    names = names.astype(jnp.int32).reshape(-1, 1)

    early = unpack_call(blocks[: len(pair_moves()[0])], transitions)
    late, total, again, weights = first_call(
        order, names, start_blocks, blocks, early, folded, shift, each
    )
    kernels = [early, late]
    again_blocks = plane_blocks(again)
    energy_part = energy_call(transform, total, my_live, energies, my_trial, norm_scale, each)

    second = second_call(
        weights, again_blocks, kernels, transform, my_live, energy_part, norm_scale, each
    )
    by_point_first = jnp.swapaxes(dense, 0, 1)
    second_blocks, row_back = pair_blocks(
        second, lambda block: row_call(order, by_point_first, start, kernels, block)
    )

    wanted_blocks = plane_blocks(after(wanted, second))
    root = first_point // col_points
    row_transform = wanted
    for step in range(1, plane_count):
        from_root = (col_index + step) % plane_count == root
        row_transform = jnp.where(from_root, wanted_blocks[step], row_transform)
    row_back = row_back.reshape(row_points, columns, transitions)
    row_part = jnp.einsum("ksv,kns->kvn", row_transform, row_back, preferred_element_type=F32)
    row_live = lax.dynamic_slice_in_dim(live, first_point, row_points, 0)
    row_energy = lax.dynamic_slice_in_dim(energies, first_point % col_points, row_points, 0)
    trial_blocks = trial.reshape(col_points, transitions, columns)
    row_trial = lax.dynamic_slice_in_dim(trial_blocks, first_point % col_points, row_points, 0)
    diagonal = jnp.where(root == col_index, row_energy[:, :, None] * row_trial.astype(F32), 0.0)
    row_part = row_part * norm_scale * row_live[:, :, None] + diagonal
    first_step = plane_sum(row_part.astype(BF16)).astype(BF16)
    first_step = first_step.reshape(row_points * transitions, columns)

    early_moves = pair_moves()[0]
    at_hand = (early_moves.index((0, 0, 0)), early_moves.index((0, 1, 0)))
    second_step = last_call(second_blocks, at_hand, order, trial, each)
    return (first_step, second_step)


def solution(mesh):
    in_specs = (
        P("pair", "pw", None),
        P("pair", "pw", None),
        P("pw", None, None),
        P("pw"),
        P("pw", None),
        P("pair", "pw", None),
        P("pair", "pw", None),
        P(),
    )
    out_specs = (P("pair", None), P("pw", None))
    return jax.shard_map(shards, mesh=mesh, in_specs=in_specs, out_specs=out_specs, check_vma=False)
```

```python
import functools
import math

import jax
import jax.numpy as jnp
from jax import lax
from jax.experimental import pallas as pl
from jax.experimental.pallas import tpu as pltpu
from jax.sharding import PartitionSpec as P

NCOND = 16
F32 = jnp.float32
BF16 = jnp.bfloat16
MIB = 1 << 20
NN = (((1,), (0,)), ((), ()))
NT = (((1,), (1,)), ((), ()))
TN = (((0,), (0,)), ((), ()))


def dot(a, b, dims=NN):
    return lax.dot_general(a, b, dims, preferred_element_type=F32)


def cost(flops, read):
    return pl.CostEstimate(flops=1, bytes_accessed=1, transcendentals=0)


def params(mib):
    return pltpu.CompilerParams(vmem_limit_bytes=mib * MIB)


def whole(shape):
    return pl.BlockSpec(shape, lambda *_: (0,) * len(shape))


ANY = pl.BlockSpec(memory_space=pl.ANY)
HBM = pl.BlockSpec(memory_space=pltpu.HBM)
VMEM = pl.BlockSpec(memory_space=pltpu.VMEM)
SMEM = pl.BlockSpec(memory_space=pltpu.SMEM)


def far(value):
    return pltpu.with_memory_space_constraint(value, pltpu.HBM)


def shaped(shape, dtype=BF16):
    return jax.ShapeDtypeStruct(shape, dtype)


def far_shaped(shape):
    return pltpu.HBM(shape, BF16)


def loads(source, target, sems, pieces, axis=0, first=0):
    size = target.shape[axis] // pieces
    copies = []
    for p in range(pieces):
        at = (slice(None),) * axis + (pl.ds(p * size, size),)
        copies.append(pltpu.make_async_copy(source.at[at], target.at[at], sems.at[first + p]))
        copies[-1].start()
    return copies


def store(source, target, at, sem, copies):
    copies.append(pltpu.make_async_copy(source.at[at], target.at[at], sem))
    copies[-1].start()


def finish(copies):
    for copy in copies:
        copy.wait()


def from_ahead(value, axis, step):
    count = lax.axis_size(axis)
    return lax.ppermute(value, axis, [((s + step) % count, s) for s in range(count)])


def flipped(value, axis, bit):
    count = lax.axis_size(axis)
    return lax.ppermute(value, axis, [(s, s ^ bit) for s in range(count)])


def plane_blocks(value):
    return [value] + [from_ahead(value, "pw", d) for d in range(1, lax.axis_size("pw"))]


def pair_moves():
    groups = lax.axis_size("pair") // 4
    far = sorted(range(groups), key=lambda d: min(d, groups - d))
    early = [(d, 0, 0) for d in far] + [(0, 1, 0)] + [(d, 0, 1) for d in far] + [(0, 1, 1)]
    early += [(d, 1, 0) for d in far[1:-1]]
    late = [(d, 1, 1) for d in far[1:-1]] + [(far[-1], 1, 0), (far[-1], 1, 1)]
    return early, late


def after(value, *others):
    return lax.optimization_barrier((value, *others))[0]


def pair_blocks(value, meanwhile=None, first=()):
    early, late = pair_moves()
    far_moves = [move for move in early if move[0] and not move[1] and not move[2]]
    held = {(0, 0, 0): value, (0, 1, 0): flipped(value, "pair", 2)}
    for move in far_moves:
        ready = value
        if meanwhile is None and move == far_moves[-1]:
            ready = after(value, *[held[other] for other in far_moves[:-1]])
        held[move] = from_ahead(ready, "pair", 4 * move[0])
    if first:
        held[far_moves[-1]] = after(held[far_moves[-1]], *first)
    done = None
    if meanwhile is not None:
        done = meanwhile(held[0, 1, 0])
        for move in far_moves:
            held[move] = after(held[move], done)
    for move in early + late:
        far, side, core = move
        if core and move not in held:
            held[move] = flipped(held[far, side, 0], "pair", 1)
        elif side and far and not core:
            held[move] = flipped(held[far, 0, 0], "pair", 2)
    return [held[move] for move in early + late], done


def pair_order():
    early, late = pair_moves()
    me = lax.axis_index("pair")
    count = lax.axis_size("pair")
    return jnp.stack([((me + 4 * far) % count) ^ (2 * side + core) for far, side, core in early + late])


def plane_sum(value):
    blocks = plane_blocks(value)
    if len(blocks) == 2:
        return blocks[0].astype(F32) + blocks[1].astype(F32)
    stacked = jnp.roll(jnp.stack(blocks), lax.axis_index("pw"), axis=0)
    return jnp.sum(stacked.astype(F32), axis=0)


def iotas(rows, cols):
    return (
        lax.broadcasted_iota(jnp.int32, (rows, cols), 0),
        lax.broadcasted_iota(jnp.int32, (rows, cols), 1),
    )


def pack(symmetric, out):
    half = symmetric.shape[0] // 2
    row, col = iotas(half, half)
    upper, lower = symmetric[:half, :half], symmetric[half:, half:]
    diagonal = jnp.sum(jnp.where(row == col, upper, 0.0), axis=0, keepdims=True)
    out[:half] = symmetric[:half, half:].astype(BF16)
    out[half : 2 * half] = jnp.where(row > col, upper, lower).astype(BF16)
    out[2 * half :] = jnp.broadcast_to(diagonal, (16, half)).astype(BF16)


def unpack(packed):
    half = packed.shape[1]
    row, col = iotas(half, half)
    corner = packed[:half]
    both = packed[half : 2 * half].astype(F32)
    diagonal = packed[2 * half : 2 * half + 1].astype(F32)
    other = both.T
    upper = jnp.where(row > col, both, jnp.where(row == col, diagonal, other))
    lower = jnp.where(row <= col, both, other)
    top = jnp.concatenate([upper.astype(BF16), corner], axis=1)
    bottom = jnp.concatenate([corner.T, lower.astype(BF16)], axis=1)
    return jnp.concatenate([top, bottom], axis=0)


def left_kernel(planes, screened_at, density, _, out, total, screened, turned, left, sems):
    pieces = sems.shape[0]
    copies = loads(screened_at.at[0], screened, sems, pieces, axis=1)
    rows = density.shape[0]
    turned[...] = density[...].T
    size = left.shape[1] // pieces
    for p in range(pieces):
        copies[p].wait()
        at = slice(p * size, (p + 1) * size)
        left[:, at] = dot(turned[...], screened[:, at]).astype(BF16)
    at = pl.multiple_of(planes[0] * rows, rows)
    total[...] = dot(left[:, pl.ds(at, rows)], density[...])
    for step in range(out.shape[0]):
        at = pl.multiple_of(planes[step + 1] * rows, rows)
        out[step] = left[:, pl.ds(at, rows)]


def left_product(planes, screened, density, later):
    rows, width = density.shape
    depth = screened.shape[2]
    return pl.pallas_call(
        left_kernel,
        in_specs=[SMEM, HBM, VMEM, ANY],
        out_specs=[VMEM, VMEM],
        out_shape=[shaped((depth // rows - 1, width, rows)), shaped((width, width), F32)],
        scratch_shapes=[
            pltpu.VMEM((rows, depth), BF16),
            pltpu.VMEM((width, rows), BF16),
            pltpu.VMEM((width, depth), BF16),
            pltpu.SemaphoreType.DMA((8,)),
        ],
        compiler_params=params(24),
        cost_estimate=cost(1, 1),
        name="left_product",
    )(planes, far(screened), density, later)


def coarse_kernel(left, total, *refs):
    *blocks, _, _, out = refs
    raw = total[...]
    for step, block in enumerate(blocks):
        raw = raw + dot(left[step], block[...])
    pack(0.5 * (raw + raw.T), out)


def coarse_block(left, total, density_blocks, later):
    width = left.shape[1]
    return pl.pallas_call(
        coarse_kernel,
        in_specs=[VMEM] * (2 + len(density_blocks)) + [ANY] * 2,
        out_specs=VMEM,
        out_shape=shaped((width + 16, width // 2)),
        compiler_params=params(16),
        cost_estimate=cost(1, 1),
        name="coarse_block",
    )(left, total, *density_blocks, *later)


def spread(table, each, same):
    rows, cols = table.shape
    tall = jnp.broadcast_to(table[:, None, :], (rows, each, cols)).reshape(rows * each, cols)
    return (tall * same).astype(BF16)


def same_column(rows, cols, each):
    row, col = iotas(rows, cols)
    return jnp.where(((row ^ col) & (each - 1)) == 0, 1.0, 0.0)


def widening(names, cols, each):
    col = lax.broadcasted_iota(jnp.int32, (names.shape[0], cols), 1)
    return jnp.where((col >= names * each) & (col < (names + 1) * each), 1.0, 0.0).astype(BF16)


def gathered_weights(order, tables, names, fine, held, out):
    rows = names.shape[0] // len(tables)
    table = jnp.concatenate([ref[ref.shape[0] - rows :, :] for ref in tables], axis=0)
    chunks = out.shape[0] // table.shape[1]
    row = lax.broadcasted_iota(jnp.int32, names.shape, 0)
    col = lax.broadcasted_iota(jnp.int32, (names.shape[0], fine), 1)
    for p in range(chunks):
        here = jnp.where(row % chunks == p, names[...], -1)
        place = jnp.where(col == here, 1.0, 0.0).astype(BF16)
        at = slice(p * table.shape[1], (p + 1) * table.shape[1])
        held[at] = dot(table, place, TN)
    points = out.shape[0] // order.shape[0]
    for c in range(order.shape[0]):
        at = pl.ds(pl.multiple_of(order[c] * points, points), points)
        out[c * points : (c + 1) * points] = held[at, :].astype(BF16)


def mix_vectors(weights, blocks, each, mixed):
    points = blocks[0].shape[0] // each
    count, _, width = mixed.shape
    for n in range(each):
        at = slice(n * points, (n + 1) * points)
        vectors = jnp.concatenate([block[at] for block in blocks], axis=0)
        value = dot(weights[...], vectors).astype(BF16)
        mixed[:, at, :] = value.reshape(count, points, width)


def through(mixed, kernel_refs):
    total, c = 0.0, 0
    for ref in kernel_refs:
        for k in range(ref.shape[0]):
            total = total + dot(mixed[c], ref[k])
            c += 1
    return total


def row_kernel(each, parts, order, table, vectors_at, *refs):
    kernels, refs = refs[:parts], refs[parts:]
    _, out, vectors, mixed, held, mixer, sems = refs
    points, columns, width = vectors.shape
    count, rows = mixed.shape[:2]
    pieces = columns // (2 * each)
    group = columns // pieces
    copies = loads(vectors_at, vectors, sems, sems.shape[0])
    names = lax.broadcasted_iota(jnp.int32, (points, 1), 0)
    cols = points * each
    wide = dot(table[...], widening(names, cols, each))
    held[...] = spread(wide, each, same_column(count * rows * each, cols, each)).astype(F32)
    size = rows * each
    for c in range(count):
        at = pl.ds(pl.multiple_of(order[c] * size, size), size)
        mixer[c * size : (c + 1) * size] = held[at, :].astype(BF16)
    finish(copies)
    for p in range(pieces):
        at = slice(p * group, (p + 1) * group)
        value = vectors[:, at, :].astype(F32).reshape(points, group // each, each, width)
        parts = []
        for g in range(group // each):
            flat = value[:, g].reshape(cols, width).astype(BF16)
            parts.append(dot(mixer[...], flat).reshape(count * rows, each, width))
        joined = jnp.concatenate(parts, axis=1).astype(BF16)
        mixed[:, :, at, :] = joined.reshape(count, rows, group, width)
    total, c = 0.0, 0
    for kernel in kernels:
        for k in range(kernel.shape[0]):
            total = total + dot(mixed[c].reshape(out.shape), kernel[k])
            c += 1
    out[...] = total.astype(BF16)


def row_call(order, mix, vectors, kernels, later):
    count, rows, points = mix.shape
    columns, width = vectors.shape[1:]
    each = 8
    return pl.pallas_call(
        functools.partial(row_kernel, each, len(kernels)),
        in_specs=[SMEM, VMEM, HBM] + [VMEM] * len(kernels) + [ANY],
        out_specs=VMEM,
        out_shape=shaped((rows * columns, width)),
        scratch_shapes=[
            pltpu.VMEM(vectors.shape, BF16),
            pltpu.VMEM((count, rows, columns, width), BF16),
            pltpu.VMEM((count * rows * each, points * each), F32),
            pltpu.VMEM((count * rows * each, points * each), BF16),
            pltpu.SemaphoreType.DMA((4,)),
        ],
        compiler_params=params(24),
        cost_estimate=cost(1, 1),
        name="row_call",
    )(order, mix.reshape(count * rows, points), far(vectors), *kernels, later)


def split_rows(rows, width):
    return pltpu.VMEM((width // 128, rows, 128), F32)


def put(ref, value, at=slice(None)):
    for h in range(ref.shape[0]):
        ref[h, at, :] = value[:, h * 128 : (h + 1) * 128]


def get(ref, at=slice(None)):
    return jnp.concatenate([ref[h, at, :] for h in range(ref.shape[0])], axis=1)


def start_kernel(each, index, pick, transform_at, trial_at, live, *refs):
    start_at, mine, my_trial, transform, trial, start, held, rows, sems = refs
    pieces = 4
    load_trial = loads(trial_at, trial, sems, pieces)
    load_transform = loads(transform_at, transform, sems, pieces, first=pieces)
    points, width, _ = transform.shape
    group = points // pieces
    at_mine = pl.ds(pl.multiple_of(index[0] * each, each), each)
    stores = []
    for p in range(pieces):
        load_trial[p].wait()
        load_transform[p].wait()
        for k in range(p * group, (p + 1) * group):
            here = slice(k * each, (k + 1) * each)
            block = trial[k * width : (k + 1) * width, :]
            turned_block = block.astype(F32).T
            vectors = turned_block * live[k : k + 1, :]
            turned = dot(vectors.astype(BF16), transform[k], NT)
            start[k] = turned.astype(BF16)
            if each % 8 == 0:
                rows[0] = turned_block
                rows[1] = turned
                my_trial[here] = rows[0, at_mine, :]
                put(held, rows[1, at_mine, :], pl.ds(k, each, stride=points))
            else:
                my_trial[here] = dot(pick[...], block, NT)
                put(held, dot(pick[...], start[k]), pl.ds(k, each, stride=points))
        store(start, start_at, pl.ds(p * group, group), sems.at[2 * pieces + p], stores)
    mine[...] = get(held).astype(BF16)
    finish(stores)


def start_call(index, pick, transform, trial, live):
    each, columns = pick.shape
    points, width, _ = transform.shape
    mine = (points * each, width)
    return pl.pallas_call(
        functools.partial(start_kernel, each),
        in_specs=[SMEM, VMEM, HBM, HBM, VMEM],
        out_specs=[HBM] + [VMEM] * 2,
        out_shape=[
            far_shaped((points, columns, width)),
            shaped(mine),
            shaped(mine, F32),
        ],
        scratch_shapes=[
            pltpu.VMEM(transform.shape, BF16),
            pltpu.VMEM(trial.shape, BF16),
            pltpu.VMEM((points, columns, width), BF16),
            split_rows(*mine),
            pltpu.VMEM((2, columns, width), F32),
            pltpu.SemaphoreType.DMA((12,)),
        ],
        compiler_params=params(16),
        cost_estimate=cost(4 * points * columns * width * width, 8 * MIB),
        name="start_call",
    )(index, pick, far(transform), far(trial), live)


def fold_kernel(scale, each, place, transform_at, live, energy, my_trial, *refs):
    folded_at, shift, wanted_at, transform, folded, sems = refs
    pieces = 4
    group = transform.shape[0] // pieces
    copies = loads(transform_at, transform, sems, pieces)
    stores = []
    for p in range(pieces):
        copies[p].wait()
        for k in range(p * group, (p + 1) * group):
            here = slice(k * each, (k + 1) * each)
            table = transform[k]
            masked = (table.astype(F32) * (scale * live[k : k + 1, :])).astype(BF16)
            folded[k] = dot(masked, table, NT).astype(BF16)
            vectors = my_trial[here] * (live[k : k + 1, :] * energy[k : k + 1, :])
            shift[here] = dot(vectors.astype(BF16), table, NT)
        store(folded, folded_at, pl.ds(p * group, group), sems.at[pieces + p], stores)
    wanted = transform.at[pl.ds(place[0], wanted_at.shape[0])]
    stores.append(pltpu.make_async_copy(wanted, wanted_at, sems.at[2 * pieces]))
    stores[-1].start()
    finish(stores)


def fold_call(place, rows, transform, live, energy, my_trial, scale, each):
    points, width, _ = transform.shape
    vectors = (points * each, width)
    return pl.pallas_call(
        functools.partial(fold_kernel, scale, each),
        in_specs=[SMEM, HBM] + [VMEM] * 3,
        out_specs=[HBM, VMEM, HBM],
        out_shape=[
            far_shaped(transform.shape),
            shaped(vectors, F32),
            far_shaped((rows, width, width)),
        ],
        scratch_shapes=[
            pltpu.VMEM(transform.shape, BF16),
            pltpu.VMEM(transform.shape, BF16),
            pltpu.SemaphoreType.DMA((9,)),
        ],
        compiler_params=params(16),
        cost_estimate=cost(3 * points * width * width * width, 8 * MIB),
        name="fold_call",
    )(place, far(transform), live, energy, my_trial)


def unpack_kernel(*refs):
    *packed, out = refs
    for c, ref in enumerate(packed):
        out[c] = unpack(ref[...])


def unpack_call(packed, width):
    return pl.pallas_call(
        unpack_kernel,
        in_specs=[VMEM] * len(packed),
        out_specs=VMEM,
        out_shape=shaped((len(packed), width, width)),
        compiler_params=params(16),
        cost_estimate=cost(1, 1),
        name="unpack_call",
    )(*packed)


def first_kernel(each, count, planes, order, names, *refs):
    blocks, refs = refs[:planes], refs[planes:]
    packed, refs = refs[:count], refs[count:]
    early, folded_at, shift, late, total, again, weights, *refs = refs
    mixed, folded, held, wide, sems = refs
    pieces = sems.shape[0]
    copies = loads(folded_at, folded, sems, pieces)
    gathered_weights(order, packed, names, weights.shape[1], wide, weights)
    mix_vectors(weights, blocks, each, mixed)
    for c in range(late.shape[0]):
        late[c] = unpack(packed[early.shape[0] + c][...])
    put(total, through(mixed, [early, late]))
    points = folded.shape[0]
    for k in range(points):
        if k % (points // pieces) == 0:
            copies[k // (points // pieces)].wait()
        rows = pl.ds(k, each, stride=points)
        value = dot(get(total, rows).astype(BF16), folded[k])
        put(held, value + shift[k * each : (k + 1) * each], rows)
    again[...] = get(held).astype(BF16)


def first_call(order, names, blocks, packed, early, folded, shift, each):
    count = len(packed)
    rows, width = blocks[0].shape
    points = rows // each
    fine = points * len(blocks)
    operands = [names, *blocks, *packed, early, far(folded), shift]
    return pl.pallas_call(
        functools.partial(first_kernel, each, count, len(blocks)),
        in_specs=[SMEM] + [VMEM] * (len(operands) - 2) + [HBM, VMEM],
        out_specs=[VMEM] * 4,
        out_shape=[
            shaped((count - early.shape[0], width, width)),
            shaped((width // 128, rows, 128), F32),
            shaped((rows, width)),
            shaped((count * points, fine)),
        ],
        scratch_shapes=[
            pltpu.VMEM((count, rows, width), BF16),
            pltpu.VMEM(folded.shape, BF16),
            split_rows(rows, width),
            pltpu.VMEM((count * points, fine), F32),
            pltpu.SemaphoreType.DMA((8,)),
        ],
        compiler_params=params(20),
        cost_estimate=cost(1, 1),
        name="first_call",
    )(order, *operands)


def energy_kernel(scale, each, transform_at, total, live, energy, trial, out, transform, sems):
    pieces = sems.shape[0]
    copies = loads(transform_at, transform, sems, pieces)
    points = transform.shape[0]
    for k in range(points):
        if k % (points // pieces) == 0:
            copies[k // (points // pieces)].wait()
        here = slice(k * each, (k + 1) * each)
        turned = dot(get(total, pl.ds(k, each, stride=points)).astype(BF16), transform[k])
        row = energy[k : k + 1, :]
        out[here] = (turned * (scale * live[k : k + 1, :]) + row * trial[here]) * row


def energy_call(transform, total, live, energy, my_trial, scale, each):
    return pl.pallas_call(
        functools.partial(energy_kernel, scale, each),
        in_specs=[HBM] + [VMEM] * 4,
        out_specs=VMEM,
        out_shape=shaped(my_trial.shape, F32),
        scratch_shapes=[pltpu.VMEM(transform.shape, BF16), pltpu.SemaphoreType.DMA((4,))],
        compiler_params=params(16),
        cost_estimate=cost(1, 1),
        name="energy_call",
    )(far(transform), total, live, energy, my_trial)


def second_kernel(scale, each, planes, weights, *refs):
    blocks, refs = refs[:planes], refs[planes:]
    early, late, transform_at, live, shift, out, mixed, transform, total, held, sems = refs
    pieces = sems.shape[0]
    copies = loads(transform_at, transform, sems, pieces)
    mix_vectors(weights, blocks, each, mixed)
    put(total, through(mixed, [early, late]))
    points = transform.shape[0]
    for k in range(points):
        if k % (points // pieces) == 0:
            copies[k // (points // pieces)].wait()
        here = slice(k * each, (k + 1) * each)
        turned = dot(get(total, pl.ds(k, each, stride=points)).astype(BF16), transform[k])
        held[here] = turned * (scale * live[k : k + 1, :]) + shift[here]
    out[...] = held[...].astype(BF16)


def second_call(weights, blocks, kernels, transform, live, shift, scale, each):
    rows, width = shift.shape
    count = sum(kernel.shape[0] for kernel in kernels)
    operands = [weights, *blocks, *kernels, far(transform), live, shift]
    return pl.pallas_call(
        functools.partial(second_kernel, scale, each, len(blocks)),
        in_specs=[VMEM] * (len(operands) - 3) + [HBM, VMEM, VMEM],
        out_specs=VMEM,
        out_shape=shaped((rows, width)),
        scratch_shapes=[
            pltpu.VMEM((count, rows, width), BF16),
            pltpu.VMEM(transform.shape, BF16),
            split_rows(rows, width),
            pltpu.VMEM((rows, width), F32),
            pltpu.SemaphoreType.DMA((8,)),
        ],
        compiler_params=params(20),
        cost_estimate=cost(1, 1),
        name="second_call",
    )(*operands)


def last_kernel(each, order, trial_at, *refs):
    *blocks, out_at, held, trial, out, in_sems, out_sems = refs
    pieces = out_sems.shape[0]
    load_trial = loads(trial_at, trial, in_sems, pieces)
    for r, block in enumerate(blocks):
        held[order[r]] = block[...]
    width, columns = held.shape[2], trial.shape[1]
    points = trial.shape[0] // width // pieces
    stores = []
    for p in range(pieces):
        load_trial[p].wait()
        part = held[:, p * points * each : (p + 1) * points * each, :].astype(F32)
        part = part.reshape(len(blocks), points, each, width)
        for k in range(points):
            rows = part[:, k].reshape(columns, width)
            first = (p * points + k) * width
            at = slice(first, first + width)
            out[at] = 2.0 * rows.T - trial[at].astype(F32)
        at = pl.ds(p * points * width, points * width)
        store(out, out_at, at, out_sems.at[p], stores)
    finish(stores)


def last_call(blocks, order, trial, each):
    total, columns = trial.shape
    rows, width = blocks[0].shape
    if each % 8 != 0:
        place = jnp.zeros_like(order).at[order].set(jnp.arange(order.shape[0], dtype=jnp.int32))
        held = jnp.stack(blocks)[place].reshape(len(blocks), -1, each, width)
        summed = jnp.transpose(held, (1, 3, 0, 2)).reshape(total, columns)
        return 2.0 * summed.astype(F32) - trial.astype(F32)
    pieces = 8
    return pl.pallas_call(
        functools.partial(last_kernel, each),
        in_specs=[SMEM, HBM] + [VMEM] * len(blocks),
        out_specs=HBM,
        out_shape=shaped((total, columns), F32),
        scratch_shapes=[
            pltpu.VMEM((len(blocks), rows, width), BF16),
            pltpu.VMEM((total, columns), BF16),
            pltpu.VMEM((total, columns), F32),
            pltpu.SemaphoreType.DMA((pieces,)),
            pltpu.SemaphoreType.DMA((pieces,)),
        ],
        compiler_params=params(24),
        cost_estimate=cost(2 * total * columns * width, 8 * MIB),
        name="last_call",
    )(order, far(trial), *blocks)


def shards(screened, density, transform, energy, trial, coarse_index, interp_weight, bands):
    pair_count = lax.axis_size("pair")
    plane_count = lax.axis_size("pw")
    row_index = lax.axis_index("pair")
    col_index = lax.axis_index("pw")
    transitions = density.shape[2]
    row_points, col_points, neighbours = coarse_index.shape
    fine_points = bands.shape[0]
    columns = trial.shape[1]
    each = columns // pair_count
    norm_scale = 1.0 / math.sqrt(fine_points * transitions)
    order = pair_order().astype(jnp.int32)

    density_blocks = plane_blocks(density[0])

    names = jnp.arange(pair_count, dtype=jnp.int32)
    hit = jnp.swapaxes(coarse_index, 1, 2)[:, None, :, :] == names[None, :, None, None]
    weight = jnp.swapaxes(interp_weight, 1, 2).astype(F32)[:, None, :, :]
    dense = jnp.sum(jnp.where(hit, weight, 0.0), axis=2).astype(BF16)

    positions = jnp.arange(transitions) % NCOND
    live = (positions[None, :] < bands[:, None]).astype(F32)
    my_live = lax.dynamic_slice_in_dim(live, col_index * col_points, col_points, 0)
    energies = energy.reshape(col_points, transitions)
    pick = (
        jnp.arange(columns)[None, :] == row_index * each + jnp.arange(each)[:, None]
    ).astype(BF16)

    start, my_start, my_trial = start_call(
        row_index[None].astype(jnp.int32), pick, transform, trial, my_live
    )

    planes = jnp.stack([(col_index + d) % plane_count for d in range(plane_count)])
    planes = planes.astype(jnp.int32)
    first_point = row_index * row_points
    place = (first_point % col_points).astype(jnp.int32)
    left, own = left_product(planes, screened, density[0], my_start)
    folded, shift, wanted = fold_call(
        place[None], row_points, transform, my_live, energies, my_trial, norm_scale, each
    )
    packed = coarse_block(left, own, density_blocks[1:], (shift, my_start))
    packed = plane_sum(packed).astype(BF16)

    table = dense.reshape(row_points, -1)
    chunks = table.shape[1] // packed.shape[1]
    table = table.reshape(row_points * chunks, packed.shape[1])
    start_blocks = plane_blocks(after(my_start, packed))
    blocks, _ = pair_blocks(jnp.concatenate([packed, table], axis=0), first=start_blocks[1:])
    names = order[:, None] * row_points + jnp.arange(row_points * chunks)[None, :] // chunks
    names = (names - col_index * col_points) % fine_points
    names = names.astype(jnp.int32).reshape(-1, 1)

    early = unpack_call(blocks[: len(pair_moves()[0])], transitions)
    late, total, again, weights = first_call(
        order, names, start_blocks, blocks, early, folded, shift, each
    )
    kernels = [early, late]
    again_blocks = plane_blocks(again)
    energy_part = energy_call(transform, total, my_live, energies, my_trial, norm_scale, each)

    second = second_call(
        weights, again_blocks, kernels, transform, my_live, energy_part, norm_scale, each
    )
    by_point_first = jnp.swapaxes(dense, 0, 1)
    second_blocks, row_back = pair_blocks(
        second, lambda block: row_call(order, by_point_first, start, kernels, block)
    )

    wanted_blocks = plane_blocks(after(wanted, second))
    root = first_point // col_points
    row_transform = wanted
    for step in range(1, plane_count):
        from_root = (col_index + step) % plane_count == root
        row_transform = jnp.where(from_root, wanted_blocks[step], row_transform)
    row_back = row_back.reshape(row_points, columns, transitions)
    row_part = jnp.einsum("ksv,kns->kvn", row_transform, row_back, preferred_element_type=F32)
    row_live = lax.dynamic_slice_in_dim(live, first_point, row_points, 0)
    row_energy = lax.dynamic_slice_in_dim(energies, first_point % col_points, row_points, 0)
    trial_blocks = trial.reshape(col_points, transitions, columns)
    row_trial = lax.dynamic_slice_in_dim(trial_blocks, first_point % col_points, row_points, 0)
    diagonal = jnp.where(root == col_index, row_energy[:, :, None] * row_trial.astype(F32), 0.0)
    row_part = row_part * norm_scale * row_live[:, :, None] + diagonal
    first_step = plane_sum(row_part.astype(BF16)).astype(BF16)
    first_step = first_step.reshape(row_points * transitions, columns)

    second_step = last_call(second_blocks, order, trial, each)
    return (first_step, second_step)


def solution(mesh):
    in_specs = (
        P("pair", "pw", None),
        P("pair", "pw", None),
        P("pw", None, None),
        P("pw"),
        P("pw", None),
        P("pair", "pw", None),
        P("pair", "pw", None),
        P(),
    )
    out_specs = (P("pair", None), P("pw", None))
    return jax.shard_map(shards, mesh=mesh, in_specs=in_specs, out_specs=out_specs, check_vma=False)
```

```python
import functools
import math

import jax
import jax.numpy as jnp
from jax import lax
from jax.experimental import pallas as pl
from jax.experimental.pallas import tpu as pltpu
from jax.sharding import PartitionSpec as P

NCOND = 16
F32 = jnp.float32
BF16 = jnp.bfloat16
MIB = 1 << 20
NN = (((1,), (0,)), ((), ()))
NT = (((1,), (1,)), ((), ()))
TN = (((0,), (0,)), ((), ()))


def dot(a, b, dims=NN):
    return lax.dot_general(a, b, dims, preferred_element_type=F32)


def cost(flops, read):
    return pl.CostEstimate(flops=1, bytes_accessed=1, transcendentals=0)


def params(mib):
    return pltpu.CompilerParams(vmem_limit_bytes=mib * MIB)


def whole(shape):
    return pl.BlockSpec(shape, lambda *_: (0,) * len(shape))


ANY = pl.BlockSpec(memory_space=pl.ANY)
HBM = pl.BlockSpec(memory_space=pltpu.HBM)
VMEM = pl.BlockSpec(memory_space=pltpu.VMEM)
SMEM = pl.BlockSpec(memory_space=pltpu.SMEM)


def far(value):
    return pltpu.with_memory_space_constraint(value, pltpu.HBM)


def shaped(shape, dtype=BF16):
    return jax.ShapeDtypeStruct(shape, dtype)


def far_shaped(shape):
    return pltpu.HBM(shape, BF16)


def loads(source, target, sems, pieces, axis=0, first=0):
    size = target.shape[axis] // pieces
    copies = []
    for p in range(pieces):
        at = (slice(None),) * axis + (pl.ds(p * size, size),)
        copies.append(pltpu.make_async_copy(source.at[at], target.at[at], sems.at[first + p]))
        copies[-1].start()
    return copies


def store(source, target, at, sem, copies):
    copies.append(pltpu.make_async_copy(source.at[at], target.at[at], sem))
    copies[-1].start()


def finish(copies):
    for copy in copies:
        copy.wait()


def from_ahead(value, axis, step):
    count = lax.axis_size(axis)
    return lax.ppermute(value, axis, [((s + step) % count, s) for s in range(count)])


def flipped(value, axis, bit):
    count = lax.axis_size(axis)
    return lax.ppermute(value, axis, [(s, s ^ bit) for s in range(count)])


def plane_blocks(value):
    return [value] + [from_ahead(value, "pw", d) for d in range(1, lax.axis_size("pw"))]


def pair_moves():
    groups = lax.axis_size("pair") // 4
    far = sorted(range(groups), key=lambda d: min(d, groups - d))
    early = [(d, 0, 0) for d in far] + [(0, 1, 0)] + [(d, 0, 1) for d in far] + [(0, 1, 1)]
    early += [(d, 1, 0) for d in far[1:-1]]
    late = [(d, 1, 1) for d in far[1:-1]] + [(far[-1], 1, 0), (far[-1], 1, 1)]
    return early, late


def after(value, *others):
    return lax.optimization_barrier((value, *others))[0]


def pair_blocks(value, meanwhile=None, first=()):
    early, late = pair_moves()
    far_moves = [move for move in early if move[0] and not move[1] and not move[2]]
    held = {(0, 0, 0): value, (0, 1, 0): flipped(value, "pair", 2)}
    for move in far_moves:
        ready = value
        if meanwhile is None and move == far_moves[-1]:
            ready = after(value, *[held[other] for other in far_moves[:-1]])
        held[move] = from_ahead(ready, "pair", 4 * move[0])
    if first:
        held[far_moves[-1]] = after(held[far_moves[-1]], *first)
    done = None
    if meanwhile is not None:
        done = meanwhile(held[0, 1, 0])
        for move in far_moves:
            held[move] = after(held[move], done)
    for move in early + late:
        far, side, core = move
        if core and move not in held:
            held[move] = flipped(held[far, side, 0], "pair", 1)
        elif side and far and not core:
            held[move] = flipped(held[far, 0, 0], "pair", 2)
    return [held[move] for move in early + late], done


def pair_order():
    early, late = pair_moves()
    me = lax.axis_index("pair")
    count = lax.axis_size("pair")
    return jnp.stack([((me + 4 * far) % count) ^ (2 * side + core) for far, side, core in early + late])


def plane_sum(value):
    blocks = plane_blocks(value)
    if len(blocks) == 2:
        return blocks[0].astype(F32) + blocks[1].astype(F32)
    stacked = jnp.roll(jnp.stack(blocks), lax.axis_index("pw"), axis=0)
    return jnp.sum(stacked.astype(F32), axis=0)


def iotas(rows, cols):
    return (
        lax.broadcasted_iota(jnp.int32, (rows, cols), 0),
        lax.broadcasted_iota(jnp.int32, (rows, cols), 1),
    )


def pack(symmetric, out):
    half = symmetric.shape[0] // 2
    row, col = iotas(half, half)
    upper, lower = symmetric[:half, :half], symmetric[half:, half:]
    diagonal = jnp.sum(jnp.where(row == col, upper, 0.0), axis=0, keepdims=True)
    out[:half] = symmetric[:half, half:].astype(BF16)
    out[half : 2 * half] = jnp.where(row > col, upper, lower).astype(BF16)
    out[2 * half :] = jnp.broadcast_to(diagonal, (16, half)).astype(BF16)


def unpack(packed):
    half = packed.shape[1]
    row, col = iotas(half, half)
    corner = packed[:half]
    both = packed[half : 2 * half].astype(F32)
    diagonal = packed[2 * half : 2 * half + 1].astype(F32)
    other = both.T
    upper = jnp.where(row > col, both, jnp.where(row == col, diagonal, other))
    lower = jnp.where(row <= col, both, other)
    top = jnp.concatenate([upper.astype(BF16), corner], axis=1)
    bottom = jnp.concatenate([corner.T, lower.astype(BF16)], axis=1)
    return jnp.concatenate([top, bottom], axis=0)


def left_kernel(planes, screened_at, density, _, out, total, screened, turned, left, sems):
    pieces = sems.shape[0]
    copies = loads(screened_at.at[0], screened, sems, pieces, axis=1)
    rows = density.shape[0]
    turned[...] = density[...].T
    size = left.shape[1] // pieces
    for p in range(pieces):
        copies[p].wait()
        at = slice(p * size, (p + 1) * size)
        left[:, at] = dot(turned[...], screened[:, at]).astype(BF16)
    at = pl.multiple_of(planes[0] * rows, rows)
    total[...] = dot(left[:, pl.ds(at, rows)], density[...])
    for step in range(out.shape[0]):
        at = pl.multiple_of(planes[step + 1] * rows, rows)
        out[step] = left[:, pl.ds(at, rows)]


def left_product(planes, screened, density, later):
    rows, width = density.shape
    depth = screened.shape[2]
    return pl.pallas_call(
        left_kernel,
        in_specs=[SMEM, HBM, VMEM, ANY],
        out_specs=[VMEM, VMEM],
        out_shape=[shaped((depth // rows - 1, width, rows)), shaped((width, width), F32)],
        scratch_shapes=[
            pltpu.VMEM((rows, depth), BF16),
            pltpu.VMEM((width, rows), BF16),
            pltpu.VMEM((width, depth), BF16),
            pltpu.SemaphoreType.DMA((8,)),
        ],
        compiler_params=params(24),
        cost_estimate=cost(1, 1),
        name="left_product",
    )(planes, far(screened), density, later)


def coarse_kernel(left, total, *refs):
    *blocks, _, _, out = refs
    raw = total[...]
    for step, block in enumerate(blocks):
        raw = raw + dot(left[step], block[...])
    pack(0.5 * (raw + raw.T), out)


def coarse_block(left, total, density_blocks, later):
    width = left.shape[1]
    return pl.pallas_call(
        coarse_kernel,
        in_specs=[VMEM] * (2 + len(density_blocks)) + [ANY] * 2,
        out_specs=VMEM,
        out_shape=shaped((width + 16, width // 2)),
        compiler_params=params(16),
        cost_estimate=cost(1, 1),
        name="coarse_block",
    )(left, total, *density_blocks, *later)


def spread(table, each, same):
    rows, cols = table.shape
    tall = jnp.broadcast_to(table[:, None, :], (rows, each, cols)).reshape(rows * each, cols)
    return (tall * same).astype(BF16)


def same_column(rows, cols, each):
    row, col = iotas(rows, cols)
    return jnp.where(((row ^ col) & (each - 1)) == 0, 1.0, 0.0)


def widening(names, cols, each):
    col = lax.broadcasted_iota(jnp.int32, (names.shape[0], cols), 1)
    return jnp.where((col >= names * each) & (col < (names + 1) * each), 1.0, 0.0).astype(BF16)


def gathered_weights(order, tables, names, fine, held, out):
    rows = names.shape[0] // len(tables)
    table = jnp.concatenate([ref[ref.shape[0] - rows :, :] for ref in tables], axis=0)
    chunks = out.shape[0] // table.shape[1]
    row = lax.broadcasted_iota(jnp.int32, names.shape, 0)
    col = lax.broadcasted_iota(jnp.int32, (names.shape[0], fine), 1)
    for p in range(chunks):
        here = jnp.where(row % chunks == p, names[...], -1)
        place = jnp.where(col == here, 1.0, 0.0).astype(BF16)
        at = slice(p * table.shape[1], (p + 1) * table.shape[1])
        held[at] = dot(table, place, TN)
    points = out.shape[0] // order.shape[0]
    for c in range(order.shape[0]):
        at = pl.ds(pl.multiple_of(order[c] * points, points), points)
        out[c * points : (c + 1) * points] = held[at, :].astype(BF16)


def mix_vectors(weights, blocks, each, mixed):
    points = blocks[0].shape[0] // each
    count, _, width = mixed.shape
    for n in range(each):
        at = slice(n * points, (n + 1) * points)
        vectors = jnp.concatenate([block[at] for block in blocks], axis=0)
        value = dot(weights[...], vectors).astype(BF16)
        mixed[:, at, :] = value.reshape(count, points, width)


def through(mixed, kernel_refs):
    total, c = 0.0, 0
    for ref in kernel_refs:
        for k in range(ref.shape[0]):
            total = total + dot(mixed[c], ref[k])
            c += 1
    return total


def row_kernel(each, parts, order, table, vectors_at, *refs):
    kernels, refs = refs[:parts], refs[parts:]
    _, out, vectors, mixed, held, mixer, sems = refs
    points, columns, width = vectors.shape
    count, rows = mixed.shape[:2]
    pieces = columns // (2 * each)
    group = columns // pieces
    copies = loads(vectors_at, vectors, sems, sems.shape[0])
    names = lax.broadcasted_iota(jnp.int32, (points, 1), 0)
    cols = points * each
    wide = dot(table[...], widening(names, cols, each))
    held[...] = spread(wide, each, same_column(count * rows * each, cols, each)).astype(F32)
    size = rows * each
    for c in range(count):
        at = pl.ds(pl.multiple_of(order[c] * size, size), size)
        mixer[c * size : (c + 1) * size] = held[at, :].astype(BF16)
    finish(copies)
    for p in range(pieces):
        at = slice(p * group, (p + 1) * group)
        value = vectors[:, at, :].astype(F32).reshape(points, group // each, each, width)
        parts = []
        for g in range(group // each):
            flat = value[:, g].reshape(cols, width).astype(BF16)
            parts.append(dot(mixer[...], flat).reshape(count * rows, each, width))
        joined = jnp.concatenate(parts, axis=1).astype(BF16)
        mixed[:, :, at, :] = joined.reshape(count, rows, group, width)
    total, c = 0.0, 0
    for kernel in kernels:
        for k in range(kernel.shape[0]):
            total = total + dot(mixed[c].reshape(out.shape), kernel[k])
            c += 1
    out[...] = total.astype(BF16)


def row_call(order, mix, vectors, kernels, later):
    count, rows, points = mix.shape
    columns, width = vectors.shape[1:]
    each = 8
    return pl.pallas_call(
        functools.partial(row_kernel, each, len(kernels)),
        in_specs=[SMEM, VMEM, HBM] + [VMEM] * len(kernels) + [ANY],
        out_specs=VMEM,
        out_shape=shaped((rows * columns, width)),
        scratch_shapes=[
            pltpu.VMEM(vectors.shape, BF16),
            pltpu.VMEM((count, rows, columns, width), BF16),
            pltpu.VMEM((count * rows * each, points * each), F32),
            pltpu.VMEM((count * rows * each, points * each), BF16),
            pltpu.SemaphoreType.DMA((4,)),
        ],
        compiler_params=params(24),
        cost_estimate=cost(1, 1),
        name="row_call",
    )(order, mix.reshape(count * rows, points), far(vectors), *kernels, later)


def split_rows(rows, width):
    return pltpu.VMEM((width // 128, rows, 128), F32)


def put(ref, value, at=slice(None)):
    for h in range(ref.shape[0]):
        ref[h, at, :] = value[:, h * 128 : (h + 1) * 128]


def get(ref, at=slice(None)):
    return jnp.concatenate([ref[h, at, :] for h in range(ref.shape[0])], axis=1)


def start_kernel(each, index, pick, transform_at, trial_at, live, *refs):
    start_at, mine, my_trial, transform, trial, start, held, rows, sems = refs
    pieces = 4
    load_trial = loads(trial_at, trial, sems, pieces)
    load_transform = loads(transform_at, transform, sems, pieces, first=pieces)
    points, width, _ = transform.shape
    group = points // pieces
    at_mine = pl.ds(pl.multiple_of(index[0] * each, each), each)
    stores = []
    for p in range(pieces):
        load_trial[p].wait()
        load_transform[p].wait()
        for k in range(p * group, (p + 1) * group):
            here = slice(k * each, (k + 1) * each)
            block = trial[k * width : (k + 1) * width, :]
            turned_block = block.astype(F32).T
            vectors = turned_block * live[k : k + 1, :]
            turned = dot(vectors.astype(BF16), transform[k], NT)
            start[k] = turned.astype(BF16)
            if each % 8 == 0:
                rows[0] = turned_block
                rows[1] = turned
                my_trial[here] = rows[0, at_mine, :]
                put(held, rows[1, at_mine, :], pl.ds(k, each, stride=points))
            else:
                my_trial[here] = dot(pick[...], block, NT)
                put(held, dot(pick[...], start[k]), pl.ds(k, each, stride=points))
        store(start, start_at, pl.ds(p * group, group), sems.at[2 * pieces + p], stores)
    mine[...] = get(held).astype(BF16)
    finish(stores)


def start_call(index, pick, transform, trial, live):
    each, columns = pick.shape
    points, width, _ = transform.shape
    mine = (points * each, width)
    return pl.pallas_call(
        functools.partial(start_kernel, each),
        in_specs=[SMEM, VMEM, HBM, HBM, VMEM],
        out_specs=[HBM] + [VMEM] * 2,
        out_shape=[
            far_shaped((points, columns, width)),
            shaped(mine),
            shaped(mine, F32),
        ],
        scratch_shapes=[
            pltpu.VMEM(transform.shape, BF16),
            pltpu.VMEM(trial.shape, BF16),
            pltpu.VMEM((points, columns, width), BF16),
            split_rows(*mine),
            pltpu.VMEM((2, columns, width), F32),
            pltpu.SemaphoreType.DMA((12,)),
        ],
        compiler_params=params(16),
        cost_estimate=cost(4 * points * columns * width * width, 8 * MIB),
        name="start_call",
    )(index, pick, far(transform), far(trial), live)


def fold_kernel(scale, each, place, transform_at, live, energy, my_trial, *refs):
    folded_at, shift, wanted_at, transform, folded, sems = refs
    pieces = 4
    group = transform.shape[0] // pieces
    copies = loads(transform_at, transform, sems, pieces)
    stores = []
    for p in range(pieces):
        copies[p].wait()
        for k in range(p * group, (p + 1) * group):
            here = slice(k * each, (k + 1) * each)
            table = transform[k]
            masked = (table.astype(F32) * (scale * live[k : k + 1, :])).astype(BF16)
            folded[k] = dot(masked, table, NT).astype(BF16)
            vectors = my_trial[here] * (live[k : k + 1, :] * energy[k : k + 1, :])
            shift[here] = dot(vectors.astype(BF16), table, NT)
        store(folded, folded_at, pl.ds(p * group, group), sems.at[pieces + p], stores)
    wanted = transform.at[pl.ds(place[0], wanted_at.shape[0])]
    stores.append(pltpu.make_async_copy(wanted, wanted_at, sems.at[2 * pieces]))
    stores[-1].start()
    finish(stores)


def fold_call(place, rows, transform, live, energy, my_trial, scale, each):
    points, width, _ = transform.shape
    vectors = (points * each, width)
    return pl.pallas_call(
        functools.partial(fold_kernel, scale, each),
        in_specs=[SMEM, HBM] + [VMEM] * 3,
        out_specs=[HBM, VMEM, HBM],
        out_shape=[
            far_shaped(transform.shape),
            shaped(vectors, F32),
            far_shaped((rows, width, width)),
        ],
        scratch_shapes=[
            pltpu.VMEM(transform.shape, BF16),
            pltpu.VMEM(transform.shape, BF16),
            pltpu.SemaphoreType.DMA((9,)),
        ],
        compiler_params=params(16),
        cost_estimate=cost(3 * points * width * width * width, 8 * MIB),
        name="fold_call",
    )(place, far(transform), live, energy, my_trial)


def unpack_kernel(*refs):
    *packed, out = refs
    for c, ref in enumerate(packed):
        out[c] = unpack(ref[...])


def unpack_call(packed, width):
    return pl.pallas_call(
        unpack_kernel,
        in_specs=[VMEM] * len(packed),
        out_specs=VMEM,
        out_shape=shaped((len(packed), width, width)),
        compiler_params=params(16),
        cost_estimate=cost(1, 1),
        name="unpack_call",
    )(*packed)


def first_kernel(each, count, planes, order, names, *refs):
    blocks, refs = refs[:planes], refs[planes:]
    packed, refs = refs[:count], refs[count:]
    early, folded_at, shift, late, total, again, weights, *refs = refs
    mixed, folded, held, wide, sems = refs
    pieces = sems.shape[0]
    copies = loads(folded_at, folded, sems, pieces)
    gathered_weights(order, packed, names, weights.shape[1], wide, weights)
    mix_vectors(weights, blocks, each, mixed)
    for c in range(late.shape[0]):
        late[c] = unpack(packed[early.shape[0] + c][...])
    put(total, through(mixed, [early, late]))
    points = folded.shape[0]
    for k in range(points):
        if k % (points // pieces) == 0:
            copies[k // (points // pieces)].wait()
        rows = pl.ds(k, each, stride=points)
        value = dot(get(total, rows).astype(BF16), folded[k])
        put(held, value + shift[k * each : (k + 1) * each], rows)
    again[...] = get(held).astype(BF16)


def first_call(order, names, blocks, packed, early, folded, shift, each):
    count = len(packed)
    rows, width = blocks[0].shape
    points = rows // each
    fine = points * len(blocks)
    operands = [names, *blocks, *packed, early, far(folded), shift]
    return pl.pallas_call(
        functools.partial(first_kernel, each, count, len(blocks)),
        in_specs=[SMEM] + [VMEM] * (len(operands) - 2) + [HBM, VMEM],
        out_specs=[VMEM] * 4,
        out_shape=[
            shaped((count - early.shape[0], width, width)),
            shaped((width // 128, rows, 128), F32),
            shaped((rows, width)),
            shaped((count * points, fine)),
        ],
        scratch_shapes=[
            pltpu.VMEM((count, rows, width), BF16),
            pltpu.VMEM(folded.shape, BF16),
            split_rows(rows, width),
            pltpu.VMEM((count * points, fine), F32),
            pltpu.SemaphoreType.DMA((8,)),
        ],
        compiler_params=params(20),
        cost_estimate=cost(1, 1),
        name="first_call",
    )(order, *operands)


def energy_kernel(scale, each, transform_at, total, live, energy, trial, out, transform, sems):
    pieces = sems.shape[0]
    copies = loads(transform_at, transform, sems, pieces)
    points = transform.shape[0]
    for k in range(points):
        if k % (points // pieces) == 0:
            copies[k // (points // pieces)].wait()
        here = slice(k * each, (k + 1) * each)
        turned = dot(get(total, pl.ds(k, each, stride=points)).astype(BF16), transform[k])
        row = energy[k : k + 1, :]
        out[here] = (turned * (scale * live[k : k + 1, :]) + row * trial[here]) * row


def energy_call(transform, total, live, energy, my_trial, scale, each):
    return pl.pallas_call(
        functools.partial(energy_kernel, scale, each),
        in_specs=[HBM] + [VMEM] * 4,
        out_specs=VMEM,
        out_shape=shaped(my_trial.shape, F32),
        scratch_shapes=[pltpu.VMEM(transform.shape, BF16), pltpu.SemaphoreType.DMA((4,))],
        compiler_params=params(16),
        cost_estimate=cost(1, 1),
        name="energy_call",
    )(far(transform), total, live, energy, my_trial)


def second_kernel(scale, each, planes, weights, *refs):
    blocks, refs = refs[:planes], refs[planes:]
    early, late, transform_at, live, shift, out, mixed, transform, total, held, sems = refs
    pieces = sems.shape[0]
    copies = loads(transform_at, transform, sems, pieces)
    mix_vectors(weights, blocks, each, mixed)
    put(total, through(mixed, [early, late]))
    points = transform.shape[0]
    for k in range(points):
        if k % (points // pieces) == 0:
            copies[k // (points // pieces)].wait()
        here = slice(k * each, (k + 1) * each)
        turned = dot(get(total, pl.ds(k, each, stride=points)).astype(BF16), transform[k])
        held[here] = turned * (scale * live[k : k + 1, :]) + shift[here]
    out[...] = held[...].astype(BF16)


def second_call(weights, blocks, kernels, transform, live, shift, scale, each):
    rows, width = shift.shape
    count = sum(kernel.shape[0] for kernel in kernels)
    operands = [weights, *blocks, *kernels, far(transform), live, shift]
    return pl.pallas_call(
        functools.partial(second_kernel, scale, each, len(blocks)),
        in_specs=[VMEM] * (len(operands) - 3) + [HBM, VMEM, VMEM],
        out_specs=VMEM,
        out_shape=shaped((rows, width)),
        scratch_shapes=[
            pltpu.VMEM((count, rows, width), BF16),
            pltpu.VMEM(transform.shape, BF16),
            split_rows(rows, width),
            pltpu.VMEM((rows, width), F32),
            pltpu.SemaphoreType.DMA((8,)),
        ],
        compiler_params=params(20),
        cost_estimate=cost(1, 1),
        name="second_call",
    )(*operands)


def last_kernel(each, order, trial_at, *refs):
    *blocks, out_at, held, trial, out, in_sems, out_sems = refs
    pieces = out_sems.shape[0]
    load_trial = loads(trial_at, trial, in_sems, pieces)
    for r, block in enumerate(blocks):
        held[order[r]] = block[...]
    width, columns = held.shape[2], trial.shape[1]
    points = trial.shape[0] // width // pieces
    stores = []
    for p in range(pieces):
        load_trial[p].wait()
        part = held[:, p * points * each : (p + 1) * points * each, :].astype(F32)
        part = part.reshape(len(blocks), points, each, width)
        for k in range(points):
            rows = part[:, k].reshape(columns, width)
            first = (p * points + k) * width
            at = slice(first, first + width)
            out[at] = 2.0 * rows.T - trial[at].astype(F32)
        at = pl.ds(p * points * width, points * width)
        store(out, out_at, at, out_sems.at[p], stores)
    finish(stores)


def last_call(blocks, order, trial, each):
    total, columns = trial.shape
    rows, width = blocks[0].shape
    if each % 8 != 0:
        place = jnp.zeros_like(order).at[order].set(jnp.arange(order.shape[0], dtype=jnp.int32))
        held = jnp.stack(blocks)[place].reshape(len(blocks), -1, each, width)
        summed = jnp.transpose(held, (1, 3, 0, 2)).reshape(total, columns)
        return 2.0 * summed.astype(F32) - trial.astype(F32)
    pieces = 16
    return pl.pallas_call(
        functools.partial(last_kernel, each),
        in_specs=[SMEM, HBM] + [VMEM] * len(blocks),
        out_specs=HBM,
        out_shape=shaped((total, columns), F32),
        scratch_shapes=[
            pltpu.VMEM((len(blocks), rows, width), BF16),
            pltpu.VMEM((total, columns), BF16),
            pltpu.VMEM((total, columns), F32),
            pltpu.SemaphoreType.DMA((pieces,)),
            pltpu.SemaphoreType.DMA((pieces,)),
        ],
        compiler_params=params(24),
        cost_estimate=cost(2 * total * columns * width, 8 * MIB),
        name="last_call",
    )(order, far(trial), *blocks)


def shards(screened, density, transform, energy, trial, coarse_index, interp_weight, bands):
    pair_count = lax.axis_size("pair")
    plane_count = lax.axis_size("pw")
    row_index = lax.axis_index("pair")
    col_index = lax.axis_index("pw")
    transitions = density.shape[2]
    row_points, col_points, neighbours = coarse_index.shape
    fine_points = bands.shape[0]
    columns = trial.shape[1]
    each = columns // pair_count
    norm_scale = 1.0 / math.sqrt(fine_points * transitions)
    order = pair_order().astype(jnp.int32)

    density_blocks = plane_blocks(density[0])

    names = jnp.arange(pair_count, dtype=jnp.int32)
    hit = jnp.swapaxes(coarse_index, 1, 2)[:, None, :, :] == names[None, :, None, None]
    weight = jnp.swapaxes(interp_weight, 1, 2).astype(F32)[:, None, :, :]
    dense = jnp.sum(jnp.where(hit, weight, 0.0), axis=2).astype(BF16)

    positions = jnp.arange(transitions) % NCOND
    live = (positions[None, :] < bands[:, None]).astype(F32)
    my_live = lax.dynamic_slice_in_dim(live, col_index * col_points, col_points, 0)
    energies = energy.reshape(col_points, transitions)
    pick = (
        jnp.arange(columns)[None, :] == row_index * each + jnp.arange(each)[:, None]
    ).astype(BF16)

    start, my_start, my_trial = start_call(
        row_index[None].astype(jnp.int32), pick, transform, trial, my_live
    )

    planes = jnp.stack([(col_index + d) % plane_count for d in range(plane_count)])
    planes = planes.astype(jnp.int32)
    first_point = row_index * row_points
    place = (first_point % col_points).astype(jnp.int32)
    left, own = left_product(planes, screened, density[0], my_start)
    folded, shift, wanted = fold_call(
        place[None], row_points, transform, my_live, energies, my_trial, norm_scale, each
    )
    packed = coarse_block(left, own, density_blocks[1:], (shift, my_start))
    packed = plane_sum(packed).astype(BF16)

    table = dense.reshape(row_points, -1)
    chunks = table.shape[1] // packed.shape[1]
    table = table.reshape(row_points * chunks, packed.shape[1])
    start_blocks = plane_blocks(after(my_start, packed))
    blocks, _ = pair_blocks(jnp.concatenate([packed, table], axis=0), first=start_blocks[1:])
    names = order[:, None] * row_points + jnp.arange(row_points * chunks)[None, :] // chunks
    names = (names - col_index * col_points) % fine_points
    names = names.astype(jnp.int32).reshape(-1, 1)

    early = unpack_call(blocks[: len(pair_moves()[0])], transitions)
    late, total, again, weights = first_call(
        order, names, start_blocks, blocks, early, folded, shift, each
    )
    kernels = [early, late]
    again_blocks = plane_blocks(again)
    energy_part = energy_call(transform, total, my_live, energies, my_trial, norm_scale, each)

    second = second_call(
        weights, again_blocks, kernels, transform, my_live, energy_part, norm_scale, each
    )
    by_point_first = jnp.swapaxes(dense, 0, 1)
    second_blocks, row_back = pair_blocks(
        second, lambda block: row_call(order, by_point_first, start, kernels, block)
    )

    wanted_blocks = plane_blocks(after(wanted, second))
    root = first_point // col_points
    row_transform = wanted
    for step in range(1, plane_count):
        from_root = (col_index + step) % plane_count == root
        row_transform = jnp.where(from_root, wanted_blocks[step], row_transform)
    row_back = row_back.reshape(row_points, columns, transitions)
    row_part = jnp.einsum("ksv,kns->kvn", row_transform, row_back, preferred_element_type=F32)
    row_live = lax.dynamic_slice_in_dim(live, first_point, row_points, 0)
    row_energy = lax.dynamic_slice_in_dim(energies, first_point % col_points, row_points, 0)
    trial_blocks = trial.reshape(col_points, transitions, columns)
    row_trial = lax.dynamic_slice_in_dim(trial_blocks, first_point % col_points, row_points, 0)
    diagonal = jnp.where(root == col_index, row_energy[:, :, None] * row_trial.astype(F32), 0.0)
    row_part = row_part * norm_scale * row_live[:, :, None] + diagonal
    first_step = plane_sum(row_part.astype(BF16)).astype(BF16)
    first_step = first_step.reshape(row_points * transitions, columns)

    second_step = last_call(second_blocks, order, trial, each)
    return (first_step, second_step)


def solution(mesh):
    in_specs = (
        P("pair", "pw", None),
        P("pair", "pw", None),
        P("pw", None, None),
        P("pw"),
        P("pw", None),
        P("pair", "pw", None),
        P("pair", "pw", None),
        P(),
    )
    out_specs = (P("pair", None), P("pw", None))
    return jax.shard_map(shards, mesh=mesh, in_specs=in_specs, out_specs=out_specs, check_vma=False)
```
